256 devices in a mesh: mpo: 4 (over y), tensor: 64 (over x, z, core).
Axes of the slice: x: 4, y: 4, z: 8, core: 2. Of those that a mesh axis runs over, the one named last changes fastest.
Arguments:
- wavefunction: float32 [4096, 128, 128], P('tensor'), may hold values from -6 to 6
- left_env: float32 [16, 64, 128, 128], P('mpo', 'tensor'), may hold values from -0.5 to 0.5
- right_env: float32 [16, 64, 128, 128], P('mpo', 'tensor'), may hold values from -0.5 to 0.5
- mpo_values: float32 [16, 16], P('mpo'), may hold values from -4 to 4
- mpo_pattern: int32 [16, 16], P('mpo'), may hold values 0 or 1
- physical: int32 [4096], P('tensor'), may hold values from 0 to 15
- right_sector: int32 [4096, 1], P('tensor'), may hold values from 0 to 63; in each aligned block of 64 rows (0 to 63, 64 to 127, ...) no two rows name the same one
- sector_size: int32 [64], P('tensor'), may hold values from 64 to 128, as said below
Outputs:
- product: float32 [4096, 128, 128], P('tensor', 'mpo')
The draws below stay inside these ranges and needn't reach their ends.
Inputs may be any that keep to these rules, and one draw needn't show every extreme that they name: `right_sector`: among the 64 blocks of one left sector (aligned runs of blocks), no right sector appears more than 1 times. `sector_size`: some sector has exactly 128 live rows.
All inputs are finite; a program needn't handle non-finite values. No bound on the sum of `mpo_pattern` on one device may be relied on, other than what follows from the above.
Results may differ from the reference program's by a relative error of at most 0.0003.
Values sent between devices are 32-bit elements; how exact they have to be, the bound alone decides.
No kernel may reach another device: no remote copies, remote signals or barrier semaphores. Data moves between devices by JAX's collectives and lax.ppermute only.
A program may use at most 128 MiB of HBM per device.

```python
import math
import jax
import jax.numpy as jnp
import numpy as np
from jax import lax

B = 128
PHYS = 16
BLK_DEV = 64
W = 16
S = 64
NBLK = 4096
CAP = 1


def draw_sector_size(key, part):
    key = jax.random.fold_in(key, 7)
    first, second = jax.random.split(key)
    sizes = jax.random.randint(first, (S,), B // 2, B + 1)
    where_full = jax.random.randint(second, (), 0, S)
    return sizes.at[where_full].set(B).astype(jnp.int32)


def touch_ends(result, rng, smallest, high):
    spot = [jax.random.randint(jax.random.fold_in(rng, axis), (), 0, length) for axis, length in enumerate(result.shape)]
    longest = result.shape.index(max(result.shape))
    beside = spot[:longest] + [(spot[longest] + 1) % result.shape[longest]] + spot[longest + 1:]
    return result.at[tuple(spot)].set(smallest).at[tuple(beside)].set(high)


def steps_of(stream_key, shape, pieces, low, top_value):
    factor_of = 1.0
    for position, parts in pieces:
        steps = jax.random.uniform(jax.random.fold_in(jax.random.fold_in(stream_key, 6), position), (parts,), jnp.float32, low / len(pieces), top_value / len(pieces))
        factor_of = factor_of * jnp.repeat(jnp.exp(steps), shape[position] // parts).reshape((-1,) + (1,) * (len(shape) - 1 - position))
    return factor_of


def shared_out(own_key, own, number, rows, amount, top, bound, lean):
    order = jax.random.permutation(own_key, amount)
    crowded, ordinary = load_shares(amount, rows * top, bound, lean, True), load_shares(amount, rows * top, bound, lean, False)
    places = jnp.arange(amount)

    def named(sizes, offset_by):
        used = int((sizes > 0).sum())
        fixed = max(1, used // 4)
        passed = fixed + (places - fixed + offset_by * (used - fixed)) % max(1, amount - fixed)
        return jnp.zeros((amount,), jnp.int32).at[order[jnp.where(places < fixed, places, passed)]].set(jnp.asarray(sizes, jnp.int32))

    sizes = jnp.where(number % 4 == 0, named(crowded, number // 4), named(ordinary, number - number // 4 - 1))
    mixed = jax.random.permutation(jax.random.fold_in(own, 3), amount)
    source_of, receiver = mixed[0:amount // 2 * 2:2], mixed[1:amount // 2 * 2:2]
    slack = jnp.minimum(sizes[source_of] - 1, bound - sizes[receiver]) // 2
    slack = jnp.where((source_of == order[0]) | (receiver == order[0]) | (sizes[receiver] == 0), 0, jnp.maximum(slack, 0))
    passed = jax.random.randint(jax.random.fold_in(own, 4), (amount // 2,), 0, 1 << 20) % (slack + 1)
    sizes = sizes.at[source_of].add(-passed).at[receiver].add(passed)
    members = jnp.searchsorted(jnp.cumsum(sizes), jnp.arange(rows * top), side="right").astype(jnp.int32)
    grid = members.reshape(top, rows).T
    grid = grid[jax.random.permutation(jax.random.fold_in(own, 1), rows)]
    offset_by = jax.random.randint(jax.random.fold_in(own, 2), (rows, 1), 0, top)
    return jnp.take_along_axis(grid, (jnp.arange(top)[None, :] + offset_by) % top, axis=1)


def load_shares(number_of, total, reach, lean, full):
    portions = [(1 << 20) // math.isqrt(standing ** lean) + 1 for standing in range(1, number_of + 1)]
    largest = reach if full else min(reach, max(-(-total // number_of), total * portions[0] // sum(portions)))
    least = 1 if total - largest >= number_of - 1 else 0
    holding, spare = [largest] + [least] * (number_of - 1), total - largest - least * (number_of - 1)
    while spare > 0:
        free = [i for i in range(1, number_of) if holding[i] < largest] or [i for i in range(1, number_of) if holding[i] < reach]
        pool, left = sum([portions[i] for i in free]), spare
        for i in free:
            more = min(reach - holding[i], max(1, left * portions[i] // pool), spare)
            holding[i] = holding[i] + more
            spare = spare - more
    return np.array(holding)


def scatter_about(stream_key, extent, spread, reach, cuts=(), held_as=jnp.bfloat16):
    values = jax.random.normal(stream_key, extent, jnp.float32) * spread
    if len(cuts) > 0:
        values = steps_of(stream_key, extent, cuts, -0.22, 0.18) * values
    return jnp.clip(values, min=-reach, max=reach).astype(held_as)


def setup_inputs(seed: int = 0) -> dict:
    keys = jax.random.split(jax.random.key(seed), 9)
    wavefunction = scatter_about(keys[0], (NBLK, B, B), 1.0, 6.0, ((0, 64),), jnp.float32)
    left_env = scatter_about(keys[1], (W, S, B, B), B ** -0.5, 0.5, ((0, 4), (1, 64)), jnp.float32)
    right_env = scatter_about(keys[2], (W, S, B, B), B ** -0.5, 0.5, ((0, 4), (1, 64)), jnp.float32)
    mpo_values = scatter_about(keys[3], (W, PHYS), 1.0, 4.0, ((0, 4),), jnp.float32)
    mpo_pattern = touch_ends((jax.random.randint(keys[4], (W, PHYS), 0, 4) < 3).astype(jnp.int32), jax.random.fold_in(keys[4], 1), 0, 1)
    physical = touch_ends(jax.random.randint(keys[5], (NBLK,), 0, PHYS), jax.random.fold_in(keys[5], 1), 0, PHYS - 1).astype(jnp.int32)
    right_sector_keys = jax.random.split(jax.random.fold_in(keys[6], 1), NBLK // BLK_DEV)
    right_sector_turns = jax.random.permutation(jax.random.fold_in(keys[6], 3), NBLK // BLK_DEV)
    right_sector = jax.vmap(lambda own, number: shared_out(jax.random.fold_in(keys[6], 2), own, number, BLK_DEV, S, 1, CAP, 2))(right_sector_keys, right_sector_turns).reshape((NBLK, 1))
    sector_size = draw_sector_size(jax.random.fold_in(keys[8], 71), 0)
    return {"wavefunction": wavefunction, "left_env": left_env, "right_env": right_env, "mpo_values": mpo_values, "mpo_pattern": mpo_pattern, "physical": physical, "right_sector": right_sector, "sector_size": sector_size}


def reference(wavefunction, left_env, right_env, mpo_values, mpo_pattern, physical, right_sector, sector_size):
    left_sector = (jnp.arange(NBLK) // BLK_DEV).astype(jnp.int32)
    right_index = right_sector[:, 0]
    weights = mpo_values * mpo_pattern.astype(jnp.float32)
    positions = jnp.arange(B)

    def one_block(items):
        block, lefts, rights, state = items
        left_rows = jnp.take(sector_size, lefts)
        right_rows = jnp.take(sector_size, rights)
        mask = ((positions[:, None] < left_rows) & (positions[None, :] < right_rows)).astype(jnp.float32)
        masked = block * mask
        coef = jnp.take(weights, state, axis=1)
        left_blocks = jnp.take(left_env, lefts, axis=1)
        right_blocks = jnp.take(right_env, rights, axis=1)
        left_part = jnp.einsum("wab,bc->wac", left_blocks, masked, precision=lax.Precision.HIGHEST) * coef[:, None, None]
        summed = jnp.einsum("wac,wdc->ad", left_part, right_blocks, precision=lax.Precision.HIGHEST)
        return summed * mask

    return lax.map(one_block, (wavefunction, left_sector, right_index, physical))
```

```python
import functools

import jax
import jax.numpy as jnp
from jax import lax
from jax.experimental import pallas as pl
from jax.experimental.pallas import tpu as pltpu
from jax.sharding import Mesh
from jax.sharding import PartitionSpec as P

NX, NZ, NC, NM = 4, 8, 2, 4
N = 128
TENSOR = ("x", "z", "c")

SYM = dict(
    own=(0, 0), zf1=(0, -1), zb1=(0, 1), zf2=(0, -2), zb2=(0, 2), zf3=(0, -3), zb3=(0, 3), z4=(0, 4),
    xf1=(-1, 0), xb1=(1, 0), x2=(2, 0), df1=(-1, 4), db1=(1, 4), d2=(2, 4),
)
ROW = (-1, 1, 2)
SET_P, SET_Q = (-1, 1, -2), (2, -3, 3)
TRIPLE = dict(
    m1f=([(d, -1) for d in ROW], [(-1, d) for d in SET_P]),
    m1b=([(d, 1) for d in ROW], [(1, d) for d in SET_P]),
    m2f=([(d, -2) for d in ROW], [(-1, d) for d in SET_Q]),
    m2b=([(d, 2) for d in ROW], [(1, d) for d in SET_Q]),
    m3f=([(d, -3) for d in ROW], [(-2, d) for d in SET_P]),
    m3b=([(d, 3) for d in ROW], [(2, d) for d in SET_Q]),
)
BATCHES = (
    ("own", "zf1", "zb1", "xf1", "xb1", "x2", "zf2", "zb2", "m1f", "m1b"),
    ("zf3", "zb3", "z4", "m2f", "m2b", "df1", "db1", "d2"),
    ("m3f", "m3b"),
)


def slots_of(names):
    slots = []
    for name in names:
        slots += [(SYM[name], SYM[name])] if name in SYM else list(zip(*TRIPLE[name]))
    return slots


def width(name):
    return 1 if name in SYM else 3


def sector(pos, core, slot):
    (x0, z0), (x1, z1) = slot
    first = core == 0
    x = (pos[1] + jnp.where(first, x0 % NX, x1 % NX)) % NX
    z = (pos[2] + jnp.where(first, z0 % NZ, z1 % NZ)) % NZ
    return (x * NZ + z) * NC + core


def invert(meta, inverse):
    def step(k, carry):
        inverse[meta[k]] = k
        return carry

    lax.fori_loop(0, NX * NZ * NC, step, 0)


def gather_kernel(meta, pos, blocks, out, inverse, sems):
    invert(meta, inverse)
    other = 1 - pos[3]
    half = NX * NZ

    def copy(j):
        return pltpu.make_async_copy(blocks.at[inverse[j * NC + other]], out.at[j], sems.at[j])

    lax.fori_loop(0, half, lambda j, c: (copy(j).start(), c)[1], 0)
    lax.fori_loop(0, half, lambda j, c: (copy(j).wait(), c)[1], 0)


def split(value):
    high = value.astype(jnp.bfloat16)
    return high, (value - high.astype(jnp.float32)).astype(jnp.bfloat16)


def dot_nt(a, b):
    return lax.dot_general(a, b, (((1,), (1,)), ((), ())), preferred_element_type=jnp.float32)


def work_kernel(names, pos, meta_own, meta_sib, values, pattern, left_own, left_sib, blocks, blocks_sib, *rest):
    count = len(names)
    arrays, rest = rest[:count], rest[count:]
    send_own, keep_own, send_sib, keep_sib = rest[:4]
    inv_own, inv_sib, sectors, right, wave, lefts, total, sem_r, sem_a, sem_b = rest[4:]
    slots = slots_of(names)
    n = len(slots)

    at = 0
    copies = []
    for name, array in zip(names, arrays):
        if width(name) == 1:
            copies.append(pltpu.make_async_copy(array, right.at[at], sem_r.at[at]))
        else:
            copies += [pltpu.make_async_copy(array.at[t], right.at[at + t], sem_r.at[at + t]) for t in range(3)]
        at += width(name)
    for copy in copies:
        copy.start()

    invert(meta_own, inv_own)
    invert(meta_sib, inv_sib)
    core = pos[3]
    for i, slot in enumerate(slots):
        sectors[i] = sector(pos, core, slot)

    def own_copy(i):
        return pltpu.make_async_copy(blocks.at[inv_own[sectors[i]]], wave.at[i, 0], sem_a.at[i])

    def sib_copy(i):
        return pltpu.make_async_copy(blocks_sib.at[sectors[i] // NC], wave.at[i, 1], sem_b.at[i])

    def start(i, carry):
        own_copy(i).start()
        sib_copy(i).start()
        return carry

    lax.fori_loop(0, n, start, 0)
    for side, ref in enumerate((left_own, left_sib)):
        for w in range(NM):
            high, low = split(ref[w])
            lefts[side, w * N:(w + 1) * N, :N] = high
            lefts[side, w * N:(w + 1) * N, N:] = low

    m = pos[0]
    zero = jnp.zeros((N, N), jnp.bfloat16)

    def step(i, carry):
        pltpu.make_async_copy(right.at[i], right.at[i], sem_r.at[i]).wait()
        own_copy(i).wait()
        sib_copy(i).wait()
        parts = []
        for side, (meta, inverse) in enumerate(((meta_own, inv_own), (meta_sib, inv_sib))):
            high, low = split(wave[i, side])
            weights = jnp.concatenate(
                [jnp.concatenate([high, low], 1), jnp.concatenate([high, zero], 1)], 0)
            both = jnp.dot(lefts[side], weights, preferred_element_type=jnp.float32)
            both = both[:, :N] + both[:, N:]
            state = meta[NX * NZ * NC + inverse[sectors[i]]]
            coef = [values[w, state] * pattern[w, state].astype(jnp.float32) for w in range(NM)]
            parts.append([split(both[w * N:(w + 1) * N] * coef[w]) for w in range(NM)])
        acc = None
        for w in range(0, NM, 2):
            high = jnp.concatenate([jnp.concatenate([parts[s][w][0], parts[s][w + 1][0]], 1) for s in range(2)], 0)
            low = jnp.concatenate([jnp.concatenate([parts[s][w][1], parts[s][w + 1][1]], 1) for s in range(2)], 0)
            r0, r1 = split(right[i, w]), split(right[i, w + 1])
            r_high = jnp.concatenate([r0[0], r1[0]], 1)
            r_low = jnp.concatenate([r0[1], r1[1]], 1)
            big = dot_nt(high, jnp.concatenate([r_high, r_low], 0))
            small = dot_nt(low, r_high)
            now = big[:, :N] + big[:, N:] + small
            acc = now if acc is None else acc + now
        total[...] = acc
        share = N // NM
        for side, (send, keep, near, far) in enumerate(((send_own, keep_own, 1, 3), (send_sib, keep_sib, 3, 1))):
            def rows(q):
                return total[pl.ds(pl.multiple_of(side * N + q * share, share), share), :]

            send[0, i] = rows(m ^ near)
            send[1, i] = rows(m ^ 2)
            keep[0, i] = rows(m)
            keep[1, i] = rows(m ^ far)
        return carry

    lax.fori_loop(0, n, step, 0)


def final_kernel(pos, meta, *rest):
    out, inverse = rest[-2:]
    invert(meta, inverse)
    core = pos[3]
    for b, names in enumerate(BATCHES):
        own0, own1, sib0, sib1 = rest[4 * b:4 * b + 4]
        for i, slot in enumerate(slots_of(names)):
            out[inverse[sector(pos, core, slot)]] = own0[i] + own1[i]
            out[inverse[sector(pos, 1 - core, slot)]] = sib0[i] + sib1[i]


SMEM = pl.BlockSpec(memory_space=pltpu.SMEM)
VMEM = pl.BlockSpec(memory_space=pltpu.VMEM)
ANY = pl.BlockSpec(memory_space=pl.ANY)


def gather_blocks(meta, pos, blocks):
    half = NX * NZ
    return pl.pallas_call(
        gather_kernel,
        out_shape=jax.ShapeDtypeStruct((half, N, N), jnp.float32),
        in_specs=[SMEM, SMEM, ANY],
        out_specs=ANY,
        scratch_shapes=[pltpu.SMEM((NX * NZ * NC,), jnp.int32), pltpu.SemaphoreType.DMA((half,))],
        cost_estimate=pl.CostEstimate(flops=0, bytes_accessed=half * N * N * 8, transcendentals=0),
        name="gather_blocks",
    )(meta, pos, blocks)


def work(names, pos, meta_own, meta_sib, values, pattern, left_own, left_sib, blocks, blocks_sib, arrays):
    n = sum(width(name) for name in names)
    piece = jax.ShapeDtypeStruct((2, n, N // NM, N), jnp.float32)
    return pl.pallas_call(
        functools.partial(work_kernel, names),
        out_shape=(piece,) * 4,
        in_specs=[SMEM] * 5 + [VMEM] * 2 + [ANY] * (2 + len(arrays)),
        out_specs=(VMEM,) * 4,
        scratch_shapes=[
            pltpu.SMEM((NX * NZ * NC,), jnp.int32),
            pltpu.SMEM((NX * NZ * NC,), jnp.int32),
            pltpu.SMEM((n,), jnp.int32),
            pltpu.VMEM((n, NM, N, N), jnp.float32),
            pltpu.VMEM((n, 2, N, N), jnp.float32),
            pltpu.VMEM((2, NM * N, 2 * N), jnp.bfloat16),
            pltpu.VMEM((2 * N, N), jnp.float32),
            pltpu.SemaphoreType.DMA((n,)),
            pltpu.SemaphoreType.DMA((n,)),
            pltpu.SemaphoreType.DMA((n,)),
        ],
        compiler_params=pltpu.CompilerParams(vmem_limit_bytes=24 * 2**20),
        cost_estimate=pl.CostEstimate(flops=n * 3 * 16 * 2 * N**3, bytes_accessed=n * 10 * N * N * 4, transcendentals=0),
        name="work",
    )(pos, meta_own, meta_sib, values, pattern, left_own, left_sib, blocks, blocks_sib, *arrays)


def finish(pos, meta, pieces):
    return pl.pallas_call(
        final_kernel,
        out_shape=jax.ShapeDtypeStruct((NX * NZ * NC, N // NM, N), jnp.float32),
        in_specs=[SMEM, SMEM] + [VMEM] * len(pieces),
        out_specs=VMEM,
        scratch_shapes=[pltpu.SMEM((NX * NZ * NC,), jnp.int32)],
        compiler_params=pltpu.CompilerParams(vmem_limit_bytes=16 * 2**20),
        name="finish",
    )(pos, meta, *pieces)


def shift(array, axis, step):
    size = {"x": NX, "z": NZ, "c": NC}[axis]
    return lax.ppermute(array, axis, [(i, (i + step) % size) for i in range(size)])


def place(x, z, c):
    return ((x % NX) * NZ + z % NZ) * NC + c


def by_core(array, step):
    pairs = []
    for x in range(NX):
        for z in range(NZ):
            pairs.append((place(x, z, 0), place(x, z + step, 0)))
            pairs.append((place(x, z, 1), place(x + step, z, 1)))
    return lax.ppermute(array, TENSOR, pairs)


def z_far(array):
    pairs = []
    for x in range(NX):
        for z in range(NZ):
            pairs.append((place(x, z, 0), place(x, z + 1, 0)))
            pairs.append((place(x, z, 1), place(x, z - 1, 1)))
    return lax.ppermute(array, TENSOR, pairs)


def body(wavefunction, left_env, right_env, mpo_values, mpo_pattern, physical, right_sector, sector_size):
    m, x, z, c = (lax.axis_index(a) for a in ("m", "x", "z", "c"))
    first = c == 0
    pos = jnp.stack([m, x, z, c]).astype(jnp.int32)
    live = jnp.arange(N, dtype=jnp.int32) < sector_size[0]
    mask = live[:, None] & live[None, :]
    own = jnp.where(mask, right_env[:, 0], 0.0)
    left = jnp.where(mask, left_env[:, 0], 0.0)
    meta = jnp.concatenate([right_sector[:, 0], physical])
    meta_sib = shift(meta, "c", 1)
    left_sib = shift(left, "c", 1)
    blocks_sib = shift(gather_blocks(meta, pos, wavefunction), "c", 1)

    got = dict(own=own)
    got["zf1"], got["zb1"] = shift(own, "z", 1), shift(own, "z", -1)
    got["xf1"], got["xb1"] = shift(own, "x", 1), shift(own, "x", -1)
    got["zf2"], got["zb2"] = shift(got["zf1"], "z", 1), shift(got["zb1"], "z", -1)
    got["x2"] = shift(got["xf1"], "x", 1)
    row = jnp.stack([got["xf1"], got["xb1"], got["x2"]])
    set_p = jnp.stack([got["zf1"], got["zb1"], got["zf2"]])
    m1 = jnp.where(first, row, set_p)
    got["m1f"], got["m1b"] = by_core(m1, 1), by_core(m1, -1)
    got["zf3"], got["zb3"] = shift(got["zf2"], "z", 1), shift(got["zb2"], "z", -1)
    set_q = jnp.stack([got["zb2"], got["zf3"], got["zb3"]])
    got["m2f"] = by_core(jnp.where(first, got["m1f"], set_q), 1)
    got["m2b"] = by_core(jnp.where(first, got["m1b"], set_q), -1)
    got["z4"] = z_far(jnp.where(first, got["zf3"], got["zb3"]))
    got["df1"], got["db1"] = shift(got["z4"], "x", 1), shift(got["z4"], "x", -1)
    got["d2"] = shift(got["db1"], "x", -1)
    got["m3f"] = by_core(jnp.where(first, got["m2f"], got["m1f"]), 1)
    got["m3b"] = by_core(got["m2b"], -1)

    near = [(i, i ^ 1) for i in range(NM)]
    far = [(i, i ^ 3) for i in range(NM)]
    straight = [(i * NC + c, i * NC + 1 - c) for i in range(NM) for c in range(NC)]
    across = [(i * NC + c, (i ^ 1) * NC + 1 - c) for i in range(NM) for c in range(NC)]
    pieces = []
    for names in BATCHES:
        send_own, keep_own, send_sib, keep_sib = work(
            names, pos, meta, meta_sib, mpo_values, mpo_pattern, left, left_sib, wavefunction, blocks_sib,
            [got[name] for name in names])
        sum_own = keep_own + lax.ppermute(send_own, "m", near)
        sum_sib = keep_sib + lax.ppermute(send_sib, "m", far)
        pieces += [
            sum_own[0],
            lax.ppermute(sum_own[1], "m", far),
            lax.ppermute(sum_sib[0], ("m", "c"), straight),
            lax.ppermute(sum_sib[1], ("m", "c"), across),
        ]
    return finish(pos, meta, pieces)


def solution(mesh):
    grid = Mesh(mesh.devices.reshape(NM, NX, NZ, NC), ("m", "x", "z", "c"))
    in_specs = (
        P(TENSOR, None, None),
        P("m", TENSOR, None, None),
        P("m", TENSOR, None, None),
        P("m", None),
        P("m", None),
        P(TENSOR),
        P(TENSOR, None),
        P(TENSOR),
    )
    out_specs = P(TENSOR, "m", None)
    return jax.shard_map(body, mesh=grid, in_specs=in_specs, out_specs=out_specs, check_vma=False)
```

```python
import functools

import jax
import jax.numpy as jnp
from jax import lax
from jax.experimental import pallas as pl
from jax.experimental.pallas import tpu as pltpu
from jax.sharding import Mesh
from jax.sharding import PartitionSpec as P

NX, NZ, NC, NM = 4, 8, 2, 4
N = 128
TENSOR = ("x", "z", "c")
HALF = NX * NZ

SYM = dict(
    own=(0, 0), zf1=(0, -1), zb1=(0, 1), zf2=(0, -2), zb2=(0, 2), zf3=(0, -3), zb3=(0, 3), z4=(0, 4),
    xf1=(-1, 0), xb1=(1, 0), x2=(2, 0), df1=(-1, 4), db1=(1, 4), d2=(2, 4),
)
STEPS = dict(
    k1f=([(-1, -1), (1, -1)], [(-1, -1), (-1, 1)]),
    k1b=([(-1, 1), (1, 1)], [(1, -1), (1, 1)]),
    k2f=([(-1, -2), (1, -2), (2, -1)], [(-1, -2), (-1, 2), (-2, -1)]),
    k2b=([(-1, 2), (1, 2), (2, 1)], [(1, -2), (1, 2), (2, 1)]),
    k3f=([(-1, -3), (1, -3), (2, -2)], [(-1, -3), (-1, 3), (-2, -2)]),
    k3b=([(-1, 3), (1, 3), (2, 2)], [(1, -3), (1, 3), (2, 2)]),
    k4f=([(2, -3)], [(-2, -3)]),
    k4b=([(2, 3)], [(2, 3)]),
)
BATCHES = (
    ("own", "zf1", "zb1", "xf1", "xb1", "zf2", "zb2", "x2", "k1f", "k1b"),
    ("zf3", "zb3", "k2f", "k2b", "z4"),
    ("k3f", "k3b", "df1", "db1"),
    ("k4f", "k4b", "d2"),
)

LIMITS = (60, 12, 12, 12)


def slots_of(names):
    slots = []
    for name in names:
        slots += [(SYM[name], SYM[name])] if name in SYM else list(zip(*STEPS[name]))
    return slots


def width(name):
    return 1 if name in SYM else len(STEPS[name][0])


def sector(pos, core, slot):
    (x0, z0), (x1, z1) = slot
    first = core == 0
    x = (pos[1] + jnp.where(first, x0 % NX, x1 % NX)) % NX
    z = (pos[2] + jnp.where(first, z0 % NZ, z1 % NZ)) % NZ
    return (x * NZ + z) * NC + core


def split(value):
    high = value.astype(jnp.bfloat16)
    return high, (value - high.astype(jnp.float32)).astype(jnp.bfloat16)


def dot_nt(a, b):
    return lax.dot_general(a, b, (((1,), (1,)), ((), ())), preferred_element_type=jnp.float32)


def work_kernel(names, pos, inverse, side_own, side_sib, blocks, blocks_sib, *rest):
    arrays, rest = dict(zip(names, rest)), rest[len(names):]
    send, keep, table, sectors, right, wave, lefts, total, sem_r, sem_a, sem_b, sem_t = rest
    slots = slots_of(names)
    n = len(slots)

    tables = []
    for side, ref in enumerate((side_own, side_sib)):
        tables.append(pltpu.make_async_copy(ref.at[NM * N:], table.at[side], sem_t.at[side]))
        tables[side].start()
    core = pos[3]
    at = 0
    for name in names:
        if width(name) == 1:
            pltpu.make_async_copy(arrays[name], right.at[at], sem_r.at[at]).start()
        else:
            for t in range(width(name)):
                pltpu.make_async_copy(arrays[name].at[t], right.at[at + t], sem_r.at[at + t]).start()
        at += width(name)
    for i, slot in enumerate(slots):
        sectors[i] = sector(pos, core, slot)

    def own_copy(i):
        return pltpu.make_async_copy(blocks.at[inverse[sectors[i]]], wave.at[i, 0], sem_a.at[i])

    def sib_copy(i):
        place = table[1, NM, sectors[i]].astype(jnp.int32)
        return pltpu.make_async_copy(blocks_sib.at[place], wave.at[i, 1], sem_b.at[i])

    tables[0].wait()
    tables[1].wait()

    def start(i, carry):
        own_copy(i).start()
        sib_copy(i).start()
        return carry

    lax.fori_loop(0, n, start, 0)
    for side, ref in enumerate((side_own, side_sib)):
        for w in range(NM):
            high, low = split(ref[w * N:(w + 1) * N])
            lefts[side, w * N:(w + 1) * N, :N] = high
            lefts[side, w * N:(w + 1) * N, N:] = low

    m = pos[0]
    zero = jnp.zeros((N, N), jnp.bfloat16)

    def step(i, carry):
        pltpu.make_async_copy(right.at[i], right.at[i], sem_r.at[i]).wait()
        own_copy(i).wait()
        sib_copy(i).wait()
        parts = []
        for side in range(2):
            high, low = split(wave[i, side])
            weights = jnp.concatenate(
                [jnp.concatenate([high, low], 1), jnp.concatenate([high, zero], 1)], 0)
            both = jnp.dot(lefts[side], weights, preferred_element_type=jnp.float32)
            both = both[:, :N] + both[:, N:]
            parts.append([split(both[w * N:(w + 1) * N] * table[side, w, sectors[i]]) for w in range(NM)])
        acc = None
        for w in range(0, NM, 2):
            high = jnp.concatenate([jnp.concatenate([parts[s][w][0], parts[s][w + 1][0]], 1) for s in range(2)], 0)
            low = jnp.concatenate([jnp.concatenate([parts[s][w][1], parts[s][w + 1][1]], 1) for s in range(2)], 0)
            r0, r1 = split(right[i, w]), split(right[i, w + 1])
            r_high = jnp.concatenate([r0[0], r1[0]], 1)
            r_low = jnp.concatenate([r0[1], r1[1]], 1)
            big = dot_nt(high, jnp.concatenate([r_high, r_low], 0))
            small = dot_nt(low, r_high)
            now = big[:, :N] + big[:, N:] + small
            acc = now if acc is None else acc + now
        total[...] = acc
        share = N // NM
        near = jnp.where(core == 0, 1, 3)
        for side in range(2):
            def rows(q):
                return total[pl.ds(pl.multiple_of(side * N + q * share, share), share), :]

            send[0, side, i] = rows(m ^ near)
            send[1, side, i] = rows(m ^ 2)
            keep[0, side, i] = rows(m)
            keep[1, side, i] = rows(m ^ near ^ 2)
        return carry

    lax.fori_loop(0, n, step, 0)


def final_kernel(batches, pos, inverse, *rest):
    out = rest[-1]
    core = pos[3]
    for b, names in enumerate(batches):
        mine, term, other = rest[3 * b:3 * b + 3]
        for i, slot in enumerate(slots_of(names)):
            out[inverse[sector(pos, core, slot)]] = mine[i] + term[i]
            out[inverse[sector(pos, 1 - core, slot)]] = other[i]


SMEM = pl.BlockSpec(memory_space=pltpu.SMEM)
VMEM = pl.BlockSpec(memory_space=pltpu.VMEM)
ANY = pl.BlockSpec(memory_space=pl.ANY)


def work(limit, names, pos, inverse, side_own, side_sib, blocks, blocks_sib, got):
    n = sum(width(name) for name in names)
    arrays = [got[name] for name in names]
    piece = jax.ShapeDtypeStruct((2, 2, n, N // NM, N), jnp.float32)
    return pl.pallas_call(
        functools.partial(work_kernel, names),
        out_shape=(piece,) * 2,
        in_specs=[SMEM] * 2 + [VMEM] * 2 + [ANY] * (2 + len(arrays)),
        out_specs=(VMEM,) * 2,
        scratch_shapes=[
            pltpu.SMEM((2, 8, N), jnp.float32),
            pltpu.SMEM((n,), jnp.int32),
            pltpu.VMEM((n, NM, N, N), jnp.float32),
            pltpu.VMEM((n, 2, N, N), jnp.float32),
            pltpu.VMEM((2, NM * N, 2 * N), jnp.bfloat16),
            pltpu.VMEM((2 * N, N), jnp.float32),
            pltpu.SemaphoreType.DMA((n,)),
            pltpu.SemaphoreType.DMA((n,)),
            pltpu.SemaphoreType.DMA((n,)),
            pltpu.SemaphoreType.DMA((2,)),
        ],
        compiler_params=pltpu.CompilerParams(vmem_limit_bytes=limit * 2**20),
        name="work",
    )(pos, inverse, side_own, side_sib, blocks, blocks_sib, *arrays)


def finish(batches, pos, inverse, pieces):
    return pl.pallas_call(
        functools.partial(final_kernel, batches),
        out_shape=jax.ShapeDtypeStruct((NX * NZ * NC, N // NM, N), jnp.float32),
        in_specs=[SMEM, SMEM] + [VMEM] * len(pieces),
        out_specs=VMEM,
        compiler_params=pltpu.CompilerParams(vmem_limit_bytes=16 * 2**20),
        name="finish",
    )(pos, inverse, *pieces)


def shift(array, axis, step):
    size = {"x": NX, "z": NZ, "c": NC}[axis]
    return lax.ppermute(array, axis, [(i, (i + step) % size) for i in range(size)])


def place(x, z, c):
    return ((x % NX) * NZ + z % NZ) * NC + c


def by_core(array, step, cores=(0, 1)):
    pairs = []
    for x in range(NX):
        for z in range(NZ):
            pairs += [(place(x, z, c), place(x + step * c, z + step * (1 - c), c)) for c in cores]
    return lax.ppermute(array, TENSOR, pairs)


def by_core_far(array, axis, length=1):
    pairs = []
    for x in range(NX):
        for z in range(NZ):
            for c, step in ((0, length), (1, -length)):
                to = place(x + step, z, c) if axis == "x" else place(x, z + step, c)
                pairs.append((place(x, z, c), to))
    return lax.ppermute(array, TENSOR, pairs)


def fence(values):
    return lax.optimization_barrier(values)


def hops(first, second):
    return [(i * NC + c, (i ^ (first, second)[c]) * NC + c) for i in range(NM) for c in range(NC)]


def halve(parts):
    send, keep = parts
    return keep + lax.ppermute(send, ("m", "c"), hops(1, 3))


def quarter(sums):
    got = lax.ppermute(sums[1], ("m", "c"), hops(3, 1))
    return sums[0, 0], got[0], sums[0, 1] + got[1]


def swap(terms):
    return terms[0], terms[1], shift(terms[2], "c", 1)


def body(wavefunction, left_env, right_env, mpo_values, mpo_pattern, physical, right_sector, sector_size):
    m, x, z, c = (lax.axis_index(a) for a in ("m", "x", "z", "c"))
    first = c == 0
    live = jnp.arange(N, dtype=jnp.int32) < sector_size[0]
    own = jnp.where(live[:, None] & live[None, :], right_env[:, 0], 0.0)

    def pick(one, two):
        return jnp.where(first, one, two)

    got = dict(own=own)

    def tie(*names):
        for name, value in zip(names, lax.optimization_barrier([got[name] for name in names])):
            got[name] = value

    def arrive(**arrays):
        got.update(arrays)

    pos = jnp.stack([m, x, z, c]).astype(jnp.int32)
    block = jnp.arange(NC * HALF, dtype=jnp.int32)
    weights = mpo_values * mpo_pattern.astype(jnp.float32)
    is_state = physical[None, :] == jnp.arange(weights.shape[1], dtype=jnp.int32)[:, None]
    coef = jnp.sum(jnp.where(is_state[None], weights[:, :, None], 0.0), axis=1)
    is_sector = right_sector == block[None, :]
    inverse = jnp.sum(jnp.where(is_sector, block[:, None], 0), axis=0)
    coef = jnp.sum(jnp.where(is_sector[None], coef[:, :, None], 0.0), axis=1)
    table = jnp.concatenate([coef, inverse.astype(jnp.float32)[None]], axis=0)
    table = jnp.pad(table, ((0, 8 - NM - 1), (0, N - NC * HALF)))
    left = jnp.where(live[:, None] & live[None, :], left_env[:, 0], 0.0).reshape(NM * N, N)
    side = jnp.concatenate([left, table], axis=0)

    def run(batch):
        return work(LIMITS[batch], BATCHES[batch], pos, inverse, side, got["side_sib"], wavefunction, got["blocks_sib"], got)

    arrive(zf1=shift(own, "z", 1), zb1=shift(own, "z", -1))
    arrive(xf1=shift(own, "x", 1), xb1=shift(own, "x", -1))
    arrive(side=side, blocks_sib=shift(wavefunction, "c", 1))
    tie("zf1", "zb1", "xf1", "xb1", "side", "blocks_sib")

    zf1, zb1, xf1, xb1 = (got[name] for name in ("zf1", "zb1", "xf1", "xb1"))
    arrive(zf2=shift(zf1, "z", 1), zb2=shift(zb1, "z", -1))
    k1 = pick(jnp.stack([xf1, xb1]), jnp.stack([zf1, zb1]))
    arrive(k1f=by_core(k1, 1), k1b=by_core(k1, -1))
    arrive(side_sib=shift(got["side"], "c", 1))
    xb1, got["side_sib"] = fence((xb1, got["side_sib"]))
    arrive(x2=shift(xb1, "x", -1))
    tie("zf2", "zb2", "x2", "k1f", "k1b")

    zf2, zb2, x2, k1f, k1b = (got[name] for name in ("zf2", "zb2", "x2", "k1f", "k1b"))
    arrive(zf3=shift(zf2, "z", 1), zb3=shift(zb2, "z", -1))
    arrive(
        k2f=by_core(pick(jnp.stack([k1f[0], k1f[1], x2]), jnp.stack([zf2, zb2, k1f[0]])), 1),
        k2b=by_core(pick(jnp.stack([k1b[0], k1b[1], x2]), jnp.stack([zf2, zb2, k1b[1]])), -1),
    )
    got["a"] = run(0)
    tie("zf3", "zb3", "k2f", "k2b", "a")

    zf3, zb3, k2f, k2b = (got[name] for name in ("zf3", "zb3", "k2f", "k2b"))
    arrive(z4=by_core_far(pick(zf3, zb3), "z"))
    arrive(
        k3f=by_core(pick(k2f, jnp.stack([zf3, zb3, k2f[0]])), 1),
        k3b=by_core(pick(k2b, jnp.stack([zf3, zb3, k2b[1]])), -1),
    )
    a = halve(got["a"])
    tie("z4")
    arrive(df1=shift(got["z4"], "x", 1), db1=shift(got["z4"], "x", -1))
    b = run(1)
    got["done"] = a, b
    tie("df1", "db1", "k3f", "k3b", "done")

    k3f, k3b = got["k3f"], got["k3b"]
    a, b = got["done"]
    arrive(d2=shift(got["df1"], "x", 1))
    arrive(k4f=by_core(pick(k3f[2], k3f[0]), 1), k4b=by_core(pick(k3b[2], k3b[1]), -1))
    d = run(2)
    a = quarter(a)
    b = halve(b)
    got["done"] = a, b, d
    tie("d2", "k4f", "k4b", "done")

    a, b, d = got["done"]
    e = run(3)
    d = halve(d)
    b = quarter(b)
    a = swap(a)
    a, b, d, e = fence((a, b, d, e))

    e = halve(e)
    d = quarter(d)
    b = swap(b)
    b, d, e = fence((b, d, e))

    e = swap(quarter(e))
    d = swap(d)
    return finish(BATCHES, pos, inverse, a + b + d + e)


def solution(mesh):
    grid = Mesh(mesh.devices.reshape(NM, NX, NZ, NC), ("m", "x", "z", "c"))
    in_specs = (
        P(TENSOR, None, None),
        P("m", TENSOR, None, None),
        P("m", TENSOR, None, None),
        P("m", None),
        P("m", None),
        P(TENSOR),
        P(TENSOR, None),
        P(TENSOR),
    )
    out_specs = P(TENSOR, "m", None)
    return jax.shard_map(body, mesh=grid, in_specs=in_specs, out_specs=out_specs, check_vma=False)
```

```python
import functools

import jax
import jax.numpy as jnp
from jax import lax
from jax.experimental import pallas as pl
from jax.experimental.pallas import tpu as pltpu
from jax.sharding import Mesh
from jax.sharding import PartitionSpec as P

NX, NZ, NC, NM = 4, 8, 2, 4
N = 128
TENSOR = ("x", "z", "c")
HALF = NX * NZ

SYM = dict(
    own=(0, 0), zf1=(0, -1), zb1=(0, 1), zf2=(0, -2), zb2=(0, 2), zf3=(0, -3), zb3=(0, 3), z4=(0, 4),
    xf1=(-1, 0), xb1=(1, 0), x2=(2, 0), df1=(-1, 4), db1=(1, 4), d2=(2, 4),
)
STEPS = dict(
    k1f=([(-1, -1), (1, -1)], [(-1, -1), (-1, 1)]),
    k1b=([(-1, 1), (1, 1)], [(1, -1), (1, 1)]),
    k2f=([(-1, -2), (1, -2), (2, -1)], [(-1, -2), (-1, 2), (-2, -1)]),
    k2b=([(-1, 2), (1, 2), (2, 1)], [(1, -2), (1, 2), (2, 1)]),
    k3f=([(-1, -3), (1, -3), (2, -2)], [(-1, 3), (-2, -2), (-1, -3)]),
    k3b=([(-1, 3), (1, 3), (2, 2)], [(1, -3), (2, 2), (1, 3)]),
    k4f=([(2, -3)], [(-2, -3)]),
    k4b=([(2, 3)], [(2, 3)]),
)
BATCHES = (
    ("own", "zf1", "zb1", "xf1", "xb1", "zf2", "zb2", "x2", "k1f", "k1b"),
    ("zf3", "zb3", "z4", "k2f", "k2b"),
    ("k3f", "k3b", "df1", "db1"),
    ("k4f", "k4b", "d2"),
)

EARLY = ("own", "zf1", "zb1", "xf1", "xb1", "x2")
LIMITS = (12, 12, 12, 12)


def slots_of(names):
    slots = []
    for name in names:
        slots += [(SYM[name], SYM[name])] if name in SYM else list(zip(*STEPS[name]))
    return slots


def width(name):
    return 1 if name in SYM else len(STEPS[name][0])


def sector(pos, core, slot):
    (x0, z0), (x1, z1) = slot
    first = core == 0
    x = (pos[1] + jnp.where(first, x0 % NX, x1 % NX)) % NX
    z = (pos[2] + jnp.where(first, z0 % NZ, z1 % NZ)) % NZ
    return (x * NZ + z) * NC + core


def split(value):
    high = value.astype(jnp.bfloat16)
    return high, (value - high.astype(jnp.float32)).astype(jnp.bfloat16)


def dot_nt(a, b):
    return lax.dot_general(a, b, (((1,), (1,)), ((), ())), preferred_element_type=jnp.float32)


def work_kernel(names, pos, inverse, side_own, side_sib, blocks, blocks_sib, *rest):
    arrays, rest = dict(zip(names, rest)), rest[len(names):]
    send, keep, table, sectors, right, wave, lefts, total, sem_r, sem_a, sem_b, sem_t = rest
    slots = slots_of(names)
    n = len(slots)

    tables = []
    for side, ref in enumerate((side_own, side_sib)):
        tables.append(pltpu.make_async_copy(ref.at[NM * N:], table.at[side], sem_t.at[side]))
        tables[side].start()
    core = pos[3]
    at = 0
    for name in names:
        if width(name) == 1:
            pltpu.make_async_copy(arrays[name], right.at[at], sem_r.at[at]).start()
        else:
            for t in range(width(name)):
                pltpu.make_async_copy(arrays[name].at[t], right.at[at + t], sem_r.at[at + t]).start()
        at += width(name)
    for i, slot in enumerate(slots):
        sectors[i] = sector(pos, core, slot)

    def own_copy(i):
        return pltpu.make_async_copy(blocks.at[inverse[sectors[i]]], wave.at[i, 0], sem_a.at[i])

    def sib_copy(i):
        place = table[1, NM, sectors[i]].astype(jnp.int32)
        return pltpu.make_async_copy(blocks_sib.at[place], wave.at[i, 1], sem_b.at[i])

    tables[0].wait()
    tables[1].wait()

    def start(i, carry):
        own_copy(i).start()
        sib_copy(i).start()
        return carry

    lax.fori_loop(0, n, start, 0)
    for side, ref in enumerate((side_own, side_sib)):
        for w in range(NM):
            high, low = split(ref[w * N:(w + 1) * N])
            lefts[side, w * N:(w + 1) * N, :N] = high
            lefts[side, w * N:(w + 1) * N, N:] = low

    m = pos[0]
    zero = jnp.zeros((N, N), jnp.bfloat16)

    def step(i, carry):
        pltpu.make_async_copy(right.at[i], right.at[i], sem_r.at[i]).wait()
        own_copy(i).wait()
        sib_copy(i).wait()
        parts = []
        for side in range(2):
            high, low = split(wave[i, side])
            weights = jnp.concatenate(
                [jnp.concatenate([high, low], 1), jnp.concatenate([high, zero], 1)], 0)
            both = jnp.dot(lefts[side], weights, preferred_element_type=jnp.float32)
            both = both[:, :N] + both[:, N:]
            parts.append([split(both[w * N:(w + 1) * N] * table[side, w, sectors[i]]) for w in range(NM)])
        acc = None
        for w in range(0, NM, 2):
            high = jnp.concatenate([jnp.concatenate([parts[s][w][0], parts[s][w + 1][0]], 1) for s in range(2)], 0)
            low = jnp.concatenate([jnp.concatenate([parts[s][w][1], parts[s][w + 1][1]], 1) for s in range(2)], 0)
            r0, r1 = split(right[i, w]), split(right[i, w + 1])
            r_high = jnp.concatenate([r0[0], r1[0]], 1)
            r_low = jnp.concatenate([r0[1], r1[1]], 1)
            big = dot_nt(high, jnp.concatenate([r_high, r_low], 0))
            small = dot_nt(low, r_high)
            now = big[:, :N] + big[:, N:] + small
            acc = now if acc is None else acc + now
        total[...] = acc
        share = N // NM
        near = jnp.where(core == 0, 1, 3)
        for side in range(2):
            def rows(q):
                return total[pl.ds(pl.multiple_of(side * N + q * share, share), share), :]

            send[0, side, i] = rows(m ^ near)
            send[1, side, i] = rows(m ^ 2)
            keep[0, side, i] = rows(m)
            keep[1, side, i] = rows(m ^ near ^ 2)
        return carry

    lax.fori_loop(0, n, step, 0)


def final_kernel(batches, pos, inverse, *rest):
    out = rest[-1]
    core = pos[3]
    for b, names in enumerate(batches):
        mine, term, other = rest[3 * b:3 * b + 3]
        for i, slot in enumerate(slots_of(names)):
            out[inverse[sector(pos, core, slot)]] = mine[i] + term[i]
            out[inverse[sector(pos, 1 - core, slot)]] = other[i]


SMEM = pl.BlockSpec(memory_space=pltpu.SMEM)
VMEM = pl.BlockSpec(memory_space=pltpu.VMEM)
ANY = pl.BlockSpec(memory_space=pl.ANY)


def in_hbm(array):
    return pltpu.with_memory_space_constraint(array, pltpu.HBM)


def work(limit, names, pos, inverse, side_own, side_sib, blocks, blocks_sib, got):
    n = sum(width(name) for name in names)
    arrays = [in_hbm(got[name]) if name in EARLY else got[name] for name in names]
    blocks, blocks_sib = in_hbm(blocks), in_hbm(blocks_sib)
    piece = jax.ShapeDtypeStruct((2, 2, n, N // NM, N), jnp.float32)
    return pl.pallas_call(
        functools.partial(work_kernel, names),
        out_shape=(piece,) * 2,
        in_specs=[SMEM] * 2 + [VMEM] * 2 + [ANY] * (2 + len(arrays)),
        out_specs=(VMEM,) * 2,
        scratch_shapes=[
            pltpu.SMEM((2, 8, N), jnp.float32),
            pltpu.SMEM((n,), jnp.int32),
            pltpu.VMEM((n, NM, N, N), jnp.float32),
            pltpu.VMEM((n, 2, N, N), jnp.float32),
            pltpu.VMEM((2, NM * N, 2 * N), jnp.bfloat16),
            pltpu.VMEM((2 * N, N), jnp.float32),
            pltpu.SemaphoreType.DMA((n,)),
            pltpu.SemaphoreType.DMA((n,)),
            pltpu.SemaphoreType.DMA((n,)),
            pltpu.SemaphoreType.DMA((2,)),
        ],
        compiler_params=pltpu.CompilerParams(vmem_limit_bytes=limit * 2**20),
        name="work",
    )(pos, inverse, side_own, side_sib, blocks, blocks_sib, *arrays)


def finish(batches, pos, inverse, pieces):
    return pl.pallas_call(
        functools.partial(final_kernel, batches),
        out_shape=jax.ShapeDtypeStruct((NX * NZ * NC, N // NM, N), jnp.float32),
        in_specs=[SMEM, SMEM] + [VMEM] * len(pieces),
        out_specs=VMEM,
        compiler_params=pltpu.CompilerParams(vmem_limit_bytes=16 * 2**20),
        name="finish",
    )(pos, inverse, *pieces)


def shift(array, axis, step):
    size = {"x": NX, "z": NZ, "c": NC}[axis]
    return lax.ppermute(array, axis, [(i, (i + step) % size) for i in range(size)])


def place(x, z, c):
    return ((x % NX) * NZ + z % NZ) * NC + c


def by_core(array, step, cores=(0, 1)):
    pairs = []
    for x in range(NX):
        for z in range(NZ):
            pairs += [(place(x, z, c), place(x + step * c, z + step * (1 - c), c)) for c in cores]
    return lax.ppermute(array, TENSOR, pairs)


def by_core_far(array, axis, length=1):
    pairs = []
    for x in range(NX):
        for z in range(NZ):
            for c, step in ((0, length), (1, -length)):
                to = place(x + step, z, c) if axis == "x" else place(x, z + step, c)
                pairs.append((place(x, z, c), to))
    return lax.ppermute(array, TENSOR, pairs)


def fence(values):
    return lax.optimization_barrier(values)


def hops(first, second):
    return [(i * NC + c, (i ^ (first, second)[c]) * NC + c) for i in range(NM) for c in range(NC)]


def halve(parts):
    send, keep = parts
    return keep + lax.ppermute(send, ("m", "c"), hops(1, 3))


def quarter(sums):
    got = lax.ppermute(sums[1], ("m", "c"), hops(3, 1))
    return sums[0, 0], got[0], sums[0, 1] + got[1]


def direct(parts):
    send, keep = parts
    one = lax.ppermute(send[0], ("m", "c"), hops(1, 3))
    two = lax.ppermute(send[1], ("m", "c"), hops(2, 2))
    three = lax.ppermute(keep[1], ("m", "c"), hops(3, 1))
    here, there = keep[0] + one, two + three
    return here[0], there[0], here[1] + there[1]


def swap(terms):
    return terms[0], terms[1], shift(terms[2], "c", 1)


def body(wavefunction, left_env, right_env, mpo_values, mpo_pattern, physical, right_sector, sector_size):
    m, x, z, c = (lax.axis_index(a) for a in ("m", "x", "z", "c"))
    first = c == 0
    live = jnp.arange(N, dtype=jnp.int32) < sector_size[0]
    own = jnp.where(live[:, None] & live[None, :], right_env[:, 0], 0.0)

    def pick(one, two):
        return jnp.where(first, one, two)

    got = dict(own=own)

    def tie(*names):
        for name, value in zip(names, lax.optimization_barrier([got[name] for name in names])):
            got[name] = value

    def arrive(**arrays):
        got.update(arrays)

    pos = jnp.stack([m, x, z, c]).astype(jnp.int32)
    block = jnp.arange(NC * HALF, dtype=jnp.int32)
    weights = mpo_values * mpo_pattern.astype(jnp.float32)
    is_state = physical[None, :] == jnp.arange(weights.shape[1], dtype=jnp.int32)[:, None]
    coef = jnp.sum(jnp.where(is_state[None], weights[:, :, None], 0.0), axis=1)
    is_sector = right_sector == block[None, :]
    inverse = jnp.sum(jnp.where(is_sector, block[:, None], 0), axis=0)
    coef = jnp.sum(jnp.where(is_sector[None], coef[:, :, None], 0.0), axis=1)
    table = jnp.concatenate([coef, inverse.astype(jnp.float32)[None]], axis=0)
    table = jnp.pad(table, ((0, 8 - NM - 1), (0, N - NC * HALF)))
    left = jnp.where(live[:, None] & live[None, :], left_env[:, 0], 0.0).reshape(NM * N, N)
    side = jnp.concatenate([left, table], axis=0)

    def run(batch):
        return work(LIMITS[batch], BATCHES[batch], pos, inverse, side, got["side_sib"], wavefunction, got["blocks_sib"], got)

    arrive(zf1=shift(own, "z", 1), zb1=shift(own, "z", -1))
    arrive(xf1=shift(own, "x", 1), xb1=shift(own, "x", -1))
    arrive(side=side, blocks_sib=shift(wavefunction, "c", 1))
    tie("zf1", "zb1", "xf1", "xb1", "side", "blocks_sib")

    zf1, zb1, xf1, xb1 = (got[name] for name in ("zf1", "zb1", "xf1", "xb1"))
    arrive(zf2=shift(zf1, "z", 1), zb2=shift(zb1, "z", -1))
    k1 = pick(jnp.stack([xf1, xb1]), jnp.stack([zf1, zb1]))
    arrive(k1f=by_core(k1, 1), k1b=by_core(k1, -1))
    arrive(side_sib=shift(got["side"], "c", 1))
    xb1, got["side_sib"] = fence((xb1, got["side_sib"]))
    arrive(x2=shift(xb1, "x", -1))
    tie("zf2", "zb2", "x2", "k1f", "k1b")

    zf2, zb2, x2, k1f, k1b = (got[name] for name in ("zf2", "zb2", "x2", "k1f", "k1b"))
    arrive(zf3=shift(zf2, "z", 1), zb3=shift(zb2, "z", -1))
    arrive(
        k2f=by_core(pick(jnp.stack([k1f[0], k1f[1], x2]), jnp.stack([zf2, zb2, k1f[0]])), 1),
        k2b=by_core(pick(jnp.stack([k1b[0], k1b[1], x2]), jnp.stack([zf2, zb2, k1b[1]])), -1),
    )
    got["a"] = run(0)
    tie("zf3", "zb3", "a")
    zf3, zb3 = got["zf3"], got["zb3"]
    arrive(z4=by_core_far(pick(zf3, zb3), "z"))
    tie("k2f", "k2b", "z4")

    k2f, k2b, z4 = (got[name] for name in ("k2f", "k2b", "z4"))
    arrive(df1=shift(z4, "x", 1), db1=shift(z4, "x", -1))
    arrive(
        k3f=by_core(pick(k2f, jnp.stack([zb3, k2f[0], zf3])), 1),
        k3b=by_core(pick(k2b, jnp.stack([zf3, k2b[1], zb3])), -1),
    )
    a = halve(got["a"])
    b = run(1)
    got["done"] = a, b
    tie("df1", "db1", "k3f", "k3b", "done")

    k3f, k3b = got["k3f"], got["k3b"]
    a, b = got["done"]
    arrive(d2=shift(got["df1"], "x", 1))
    arrive(k4f=by_core(k3f[2], 1), k4b=by_core(k3b[2], -1))
    d = run(2)
    b = halve(b)
    got["done"] = b, d
    tie("d2", "k4f", "k4b", "done")

    b, d = got["done"]
    e = run(3)
    d = halve(d)
    a = quarter(a)
    a, d, e = fence((a, d, e))

    e = direct(e)
    b = quarter(b)
    d = quarter(d)
    a, b, d, e = fence((a, b, d, e))
    a, b, d, e = (swap(part) for part in (a, b, d, e))
    return finish(BATCHES, pos, inverse, a + b + d + e)


def solution(mesh):
    grid = Mesh(mesh.devices.reshape(NM, NX, NZ, NC), ("m", "x", "z", "c"))
    in_specs = (
        P(TENSOR, None, None),
        P("m", TENSOR, None, None),
        P("m", TENSOR, None, None),
        P("m", None),
        P("m", None),
        P(TENSOR),
        P(TENSOR, None),
        P(TENSOR),
    )
    out_specs = P(TENSOR, "m", None)
    return jax.shard_map(body, mesh=grid, in_specs=in_specs, out_specs=out_specs, check_vma=False)
```

```python
import functools

import jax
import jax.numpy as jnp
from jax import lax
from jax.experimental import pallas as pl
from jax.experimental.pallas import tpu as pltpu
from jax.sharding import Mesh
from jax.sharding import PartitionSpec as P

NX, NZ, NC, NM = 4, 8, 2, 4
N = 128
TENSOR = ("x", "z", "c")
HALF = NX * NZ

SYM = dict(
    own=(0, 0), zf1=(0, -1), zb1=(0, 1), zf2=(0, -2), zb2=(0, 2), zf3=(0, -3), zb3=(0, 3), z4=(0, 4),
    xf1=(-1, 0), xb1=(1, 0), x2=(2, 0), df1=(-1, 4), db1=(1, 4), d2=(2, 4),
)
STEPS = dict(
    k1f=([(-1, -1), (1, -1)], [(-1, -1), (-1, 1)]),
    k1b=([(-1, 1), (1, 1)], [(1, -1), (1, 1)]),
    k2f=([(-1, -2), (1, -2), (2, -1)], [(-1, -2), (-1, 2), (-2, -1)]),
    k2b=([(-1, 2), (1, 2), (2, 1)], [(1, -2), (1, 2), (2, 1)]),
    k3f=([(-1, -3), (1, -3), (2, -2)], [(-1, 3), (-2, -2), (-1, -3)]),
    k3b=([(-1, 3), (1, 3), (2, 2)], [(1, -3), (2, 2), (1, 3)]),
    k4f=([(2, -3)], [(-2, -3)]),
    k4b=([(2, 3)], [(2, 3)]),
)
BATCHES = (
    ("own", "zf1", "zb1", "xf1", "xb1", "zf2", "zb2", "x2", "k1f", "k1b"),
    ("zf3", "zb3", "z4", "k2f", "k2b"),
    ("k3f", "k3b", "df1", "db1"),
    ("k4f", "k4b", "d2"),
)

EARLY = ("own", "zf1", "zb1", "xf1", "xb1", "x2", "zf2", "zb2", "k1f", "k1b")
LIMITS = (12, 12, 12, 12)


def slots_of(names):
    slots = []
    for name in names:
        slots += [(SYM[name], SYM[name])] if name in SYM else list(zip(*STEPS[name]))
    return slots


def width(name):
    return 1 if name in SYM else len(STEPS[name][0])


def sector(pos, core, slot):
    (x0, z0), (x1, z1) = slot
    first = core == 0
    x = (pos[1] + jnp.where(first, x0 % NX, x1 % NX)) % NX
    z = (pos[2] + jnp.where(first, z0 % NZ, z1 % NZ)) % NZ
    return (x * NZ + z) * NC + core


def split(value):
    high = value.astype(jnp.bfloat16)
    return high, (value - high.astype(jnp.float32)).astype(jnp.bfloat16)


def dot_nt(a, b):
    return lax.dot_general(a, b, (((1,), (1,)), ((), ())), preferred_element_type=jnp.float32)


def work_kernel(names, pos, inverse, side_own, side_sib, blocks, blocks_sib, *rest):
    arrays, rest = dict(zip(names, rest)), rest[len(names):]
    send, keep, table, sectors, right, wave, lefts, total, sem_r, sem_a, sem_b, sem_t = rest
    slots = slots_of(names)
    n = len(slots)

    tables = []
    for side, ref in enumerate((side_own, side_sib)):
        tables.append(pltpu.make_async_copy(ref.at[NM * N:], table.at[side], sem_t.at[side]))
        tables[side].start()
    core = pos[3]
    at = 0
    for name in names:
        if width(name) == 1:
            pltpu.make_async_copy(arrays[name], right.at[at], sem_r.at[at]).start()
        else:
            for t in range(width(name)):
                pltpu.make_async_copy(arrays[name].at[t], right.at[at + t], sem_r.at[at + t]).start()
        at += width(name)
    for i, slot in enumerate(slots):
        sectors[i] = sector(pos, core, slot)

    def own_copy(i):
        return pltpu.make_async_copy(blocks.at[inverse[sectors[i]]], wave.at[i, 0], sem_a.at[i])

    def sib_copy(i):
        place = table[1, NM, sectors[i]].astype(jnp.int32)
        return pltpu.make_async_copy(blocks_sib.at[place], wave.at[i, 1], sem_b.at[i])

    def start_own(i, carry):
        own_copy(i).start()
        return carry

    def start_sib(i, carry):
        sib_copy(i).start()
        return carry

    lax.fori_loop(0, n, start_own, 0)
    tables[1].wait()
    lax.fori_loop(0, n, start_sib, 0)
    for side, ref in enumerate((side_own, side_sib)):
        for w in range(NM):
            high, low = split(ref[w * N:(w + 1) * N])
            lefts[side, w * N:(w + 1) * N, :N] = high
            lefts[side, w * N:(w + 1) * N, N:] = low
    tables[0].wait()

    m = pos[0]
    zero = jnp.zeros((N, N), jnp.bfloat16)

    def step(i, carry):
        pltpu.make_async_copy(right.at[i], right.at[i], sem_r.at[i]).wait()
        own_copy(i).wait()
        sib_copy(i).wait()
        parts = []
        for side in range(2):
            high, low = split(wave[i, side])
            weights = jnp.concatenate(
                [jnp.concatenate([high, low], 1), jnp.concatenate([high, zero], 1)], 0)
            both = jnp.dot(lefts[side], weights, preferred_element_type=jnp.float32)
            both = both[:, :N] + both[:, N:]
            parts.append([split(both[w * N:(w + 1) * N] * table[side, w, sectors[i]]) for w in range(NM)])
        acc = None
        for w in range(0, NM, 2):
            high = jnp.concatenate([jnp.concatenate([parts[s][w][0], parts[s][w + 1][0]], 1) for s in range(2)], 0)
            low = jnp.concatenate([jnp.concatenate([parts[s][w][1], parts[s][w + 1][1]], 1) for s in range(2)], 0)
            r0, r1 = split(right[i, w]), split(right[i, w + 1])
            r_high = jnp.concatenate([r0[0], r1[0]], 1)
            r_low = jnp.concatenate([r0[1], r1[1]], 1)
            big = dot_nt(high, jnp.concatenate([r_high, r_low], 0))
            small = dot_nt(low, r_high)
            now = big[:, :N] + big[:, N:] + small
            acc = now if acc is None else acc + now
        total[...] = acc
        share = N // NM
        near = jnp.where(core == 0, 1, 3)
        for side in range(2):
            def rows(q):
                return total[pl.ds(pl.multiple_of(side * N + q * share, share), share), :]

            send[0, side, i] = rows(m ^ near)
            send[1, side, i] = rows(m ^ 2)
            keep[0, side, i] = rows(m)
            keep[1, side, i] = rows(m ^ near ^ 2)
        return carry

    lax.fori_loop(0, n, step, 0)


def final_kernel(batches, pos, inverse, *rest):
    out = rest[-1]
    core = pos[3]
    others = rest[-2]
    at = 0
    for b, names in enumerate(batches):
        mine, term = rest[2 * b:2 * b + 2]
        for i, slot in enumerate(slots_of(names)):
            out[inverse[sector(pos, core, slot)]] = mine[i] + term[i]
            out[inverse[sector(pos, 1 - core, slot)]] = others[at]
            at += 1


SMEM = pl.BlockSpec(memory_space=pltpu.SMEM)
VMEM = pl.BlockSpec(memory_space=pltpu.VMEM)
ANY = pl.BlockSpec(memory_space=pl.ANY)


def in_hbm(array):
    return pltpu.with_memory_space_constraint(array, pltpu.HBM)


def work(limit, names, pos, inverse, side_own, side_sib, blocks, blocks_sib, got):
    n = sum(width(name) for name in names)
    arrays = [in_hbm(got[name]) if name in EARLY else got[name] for name in names]
    blocks, blocks_sib = in_hbm(blocks), in_hbm(blocks_sib)
    piece = jax.ShapeDtypeStruct((2, 2, n, N // NM, N), jnp.float32)
    return pl.pallas_call(
        functools.partial(work_kernel, names),
        out_shape=(piece,) * 2,
        in_specs=[SMEM] * 2 + [VMEM] * 2 + [ANY] * (2 + len(arrays)),
        out_specs=(VMEM,) * 2,
        scratch_shapes=[
            pltpu.SMEM((2, 8, N), jnp.float32),
            pltpu.SMEM((n,), jnp.int32),
            pltpu.VMEM((n, NM, N, N), jnp.float32),
            pltpu.VMEM((n, 2, N, N), jnp.float32),
            pltpu.VMEM((2, NM * N, 2 * N), jnp.bfloat16),
            pltpu.VMEM((2 * N, N), jnp.float32),
            pltpu.SemaphoreType.DMA((n,)),
            pltpu.SemaphoreType.DMA((n,)),
            pltpu.SemaphoreType.DMA((n,)),
            pltpu.SemaphoreType.DMA((2,)),
        ],
        compiler_params=pltpu.CompilerParams(vmem_limit_bytes=limit * 2**20),
        name="work",
    )(pos, inverse, side_own, side_sib, blocks, blocks_sib, *arrays)


def finish(batches, pos, inverse, pieces):
    return pl.pallas_call(
        functools.partial(final_kernel, batches),
        out_shape=jax.ShapeDtypeStruct((NX * NZ * NC, N // NM, N), jnp.float32),
        in_specs=[SMEM, SMEM] + [VMEM] * len(pieces),
        out_specs=VMEM,
        compiler_params=pltpu.CompilerParams(vmem_limit_bytes=16 * 2**20),
        name="finish",
    )(pos, inverse, *pieces)


def shift(array, axis, step):
    size = {"x": NX, "z": NZ, "c": NC}[axis]
    return lax.ppermute(array, axis, [(i, (i + step) % size) for i in range(size)])


def place(x, z, c):
    return ((x % NX) * NZ + z % NZ) * NC + c


def by_core(array, step, cores=(0, 1)):
    pairs = []
    for x in range(NX):
        for z in range(NZ):
            pairs += [(place(x, z, c), place(x + step * c, z + step * (1 - c), c)) for c in cores]
    return lax.ppermute(array, TENSOR, pairs)


def by_core_far(array, axis, length=1):
    pairs = []
    for x in range(NX):
        for z in range(NZ):
            for c, step in ((0, length), (1, -length)):
                to = place(x + step, z, c) if axis == "x" else place(x, z + step, c)
                pairs.append((place(x, z, c), to))
    return lax.ppermute(array, TENSOR, pairs)


def fence(values):
    return lax.optimization_barrier(values)


def hops(first, second):
    return [(i * NC + c, (i ^ (first, second)[c]) * NC + c) for i in range(NM) for c in range(NC)]


def halve(parts):
    send, keep = parts
    return keep + lax.ppermute(send, ("m", "c"), hops(1, 3))


def quarter(sums):
    got = lax.ppermute(sums[1], ("m", "c"), hops(3, 1))
    return sums[0, 0], got[0], sums[0, 1] + got[1]


def direct(parts):
    send, keep = parts
    one = lax.ppermute(send[0], ("m", "c"), hops(1, 3))
    two = lax.ppermute(send[1], ("m", "c"), hops(2, 2))
    three = lax.ppermute(keep[1], ("m", "c"), hops(3, 1))
    here, there = keep[0] + one, two + three
    return here[0], there[0], here[1] + there[1]


def body(wavefunction, left_env, right_env, mpo_values, mpo_pattern, physical, right_sector, sector_size):
    m, x, z, c = (lax.axis_index(a) for a in ("m", "x", "z", "c"))
    first = c == 0
    live = jnp.arange(N, dtype=jnp.int32) < sector_size[0]
    own = jnp.where(live[:, None] & live[None, :], right_env[:, 0], 0.0)

    def pick(one, two):
        return jnp.where(first, one, two)

    got = dict(own=own)

    def tie(*names):
        for name, value in zip(names, lax.optimization_barrier([got[name] for name in names])):
            got[name] = value

    def arrive(**arrays):
        got.update(arrays)

    pos = jnp.stack([m, x, z, c]).astype(jnp.int32)
    block = jnp.arange(NC * HALF, dtype=jnp.int32)
    weights = mpo_values * mpo_pattern.astype(jnp.float32)
    is_state = physical[None, :] == jnp.arange(weights.shape[1], dtype=jnp.int32)[:, None]
    coef = jnp.sum(jnp.where(is_state[None], weights[:, :, None], 0.0), axis=1)
    is_sector = right_sector == block[None, :]
    inverse = jnp.sum(jnp.where(is_sector, block[:, None], 0), axis=0)
    coef = jnp.sum(jnp.where(is_sector[None], coef[:, :, None], 0.0), axis=1)
    table = jnp.concatenate([coef, inverse.astype(jnp.float32)[None]], axis=0)
    table = jnp.pad(table, ((0, 8 - NM - 1), (0, N - NC * HALF)))
    left = jnp.where(live[:, None] & live[None, :], left_env[:, 0], 0.0).reshape(NM * N, N)
    side = jnp.concatenate([left, table], axis=0)

    def run(batch):
        return work(LIMITS[batch], BATCHES[batch], pos, inverse, side, got["side_sib"], wavefunction, got["blocks_sib"], got)

    arrive(zf1=shift(own, "z", 1), zb1=shift(own, "z", -1))
    arrive(xf1=shift(own, "x", 1), xb1=shift(own, "x", -1))
    arrive(side=side, blocks_sib=shift(wavefunction, "c", 1))
    tie("zf1", "zb1", "xf1", "xb1", "side", "blocks_sib")

    zf1, zb1, xf1, xb1 = (got[name] for name in ("zf1", "zb1", "xf1", "xb1"))
    arrive(zf2=shift(zf1, "z", 1), zb2=shift(zb1, "z", -1))
    k1 = pick(jnp.stack([xf1, xb1]), jnp.stack([zf1, zb1]))
    arrive(k1f=by_core(k1, 1), k1b=by_core(k1, -1))
    arrive(side_sib=shift(got["side"], "c", 1))
    xb1, got["side_sib"] = fence((xb1, got["side_sib"]))
    arrive(x2=shift(xb1, "x", -1))
    tie("zf2", "zb2", "x2", "k1f", "k1b")

    zf2, zb2, x2, k1f, k1b = (got[name] for name in ("zf2", "zb2", "x2", "k1f", "k1b"))
    arrive(zf3=shift(zf2, "z", 1), zb3=shift(zb2, "z", -1))
    arrive(
        k2f=by_core(pick(jnp.stack([k1f[0], k1f[1], x2]), jnp.stack([zf2, zb2, k1f[0]])), 1),
        k2b=by_core(pick(jnp.stack([k1b[0], k1b[1], x2]), jnp.stack([zf2, zb2, k1b[1]])), -1),
    )
    got["a"] = run(0)
    tie("zf3", "zb3", "a")
    zf3, zb3 = got["zf3"], got["zb3"]
    arrive(z4=by_core_far(pick(zf3, zb3), "z"))
    tie("k2f", "k2b", "z4")

    k2f, k2b, z4 = (got[name] for name in ("k2f", "k2b", "z4"))
    arrive(df1=shift(z4, "x", 1), db1=shift(z4, "x", -1))
    arrive(
        k3f=by_core(pick(k2f, jnp.stack([zb3, k2f[0], zf3])), 1),
        k3b=by_core(pick(k2b, jnp.stack([zf3, k2b[1], zb3])), -1),
    )
    a = halve(got["a"])
    b = run(1)
    got["done"] = a, b
    tie("df1", "db1", "k3f", "k3b", "done")

    k3f, k3b = got["k3f"], got["k3b"]
    a, b = got["done"]
    arrive(d2=shift(got["df1"], "x", 1))
    arrive(k4f=by_core(k3f[2], 1), k4b=by_core(k3b[2], -1))
    d = run(2)
    b = halve(b)
    got["done"] = b, d
    tie("d2", "k4f", "k4b", "done")

    b, d = got["done"]
    e = run(3)
    d = halve(d)
    a = quarter(a)
    a, d, e = fence((a, d, e))

    e = direct(e)
    b = quarter(b)
    d = quarter(d)
    a, b, d, e = fence((a, b, d, e))
    others = shift(jnp.concatenate([part[2] for part in (a, b, d, e)]), "c", 1)
    return finish(BATCHES, pos, inverse, a[:2] + b[:2] + d[:2] + e[:2] + (others,))


def solution(mesh):
    grid = Mesh(mesh.devices.reshape(NM, NX, NZ, NC), ("m", "x", "z", "c"))
    in_specs = (
        P(TENSOR, None, None),
        P("m", TENSOR, None, None),
        P("m", TENSOR, None, None),
        P("m", None),
        P("m", None),
        P(TENSOR),
        P(TENSOR, None),
        P(TENSOR),
    )
    out_specs = P(TENSOR, "m", None)
    return jax.shard_map(body, mesh=grid, in_specs=in_specs, out_specs=out_specs, check_vma=False)
```

```python
import functools

import jax
import jax.numpy as jnp
from jax import lax
from jax.experimental import pallas as pl
from jax.experimental.pallas import tpu as pltpu
from jax.sharding import Mesh
from jax.sharding import PartitionSpec as P

NX, NZ, NC, NM = 4, 8, 2, 4
N = 128
TENSOR = ("x", "z", "c")
HALF = NX * NZ

SYM = dict(
    own=(0, 0), zf1=(0, -1), zb1=(0, 1), zf2=(0, -2), zb2=(0, 2), zf3=(0, -3), zb3=(0, 3), z4=(0, 4),
    xf1=(-1, 0), xb1=(1, 0), x2=(2, 0), df1=(-1, 4), db1=(1, 4), d2=(2, 4),
)
STEPS = dict(
    k1f=([(-1, -1), (1, -1)], [(-1, -1), (-1, 1)]),
    k1b=([(-1, 1), (1, 1)], [(1, -1), (1, 1)]),
    k2f=([(-1, -2), (1, -2), (2, -1)], [(-1, -2), (-1, 2), (-2, -1)]),
    k2b=([(-1, 2), (1, 2), (2, 1)], [(1, -2), (1, 2), (2, 1)]),
    k3f=([(-1, -3), (1, -3), (2, -2)], [(-1, 3), (-2, -2), (-1, -3)]),
    k3b=([(-1, 3), (1, 3), (2, 2)], [(1, -3), (2, 2), (1, 3)]),
    k4f=([(2, -3)], [(-2, -3)]),
    k4b=([(2, 3)], [(2, 3)]),
)
BATCHES = (
    ("own", "zf1", "zb1", "xf1", "xb1", "zf2", "zb2", "x2", "k1f", "k1b"),
    ("zf3", "zb3", "z4", "k2f", "k2b"),
    ("k3f", "k3b", "df1", "db1"),
    ("k4f", "k4b", "d2"),
)

EARLY = ("own", "zf1", "zb1", "xf1", "xb1", "x2", "zf2", "zb2", "k1f", "k1b")
LIMITS = (12, 12, 12, 12)


def slots_of(names):
    slots = []
    for name in names:
        slots += [(SYM[name], SYM[name])] if name in SYM else list(zip(*STEPS[name]))
    return slots


def width(name):
    return 1 if name in SYM else len(STEPS[name][0])


def sector(pos, core, slot):
    (x0, z0), (x1, z1) = slot
    first = core == 0
    x = (pos[1] + jnp.where(first, x0 % NX, x1 % NX)) % NX
    z = (pos[2] + jnp.where(first, z0 % NZ, z1 % NZ)) % NZ
    return (x * NZ + z) * NC + core


def split(value):
    high = value.astype(jnp.bfloat16)
    return high, (value - high.astype(jnp.float32)).astype(jnp.bfloat16)


def dot_nt(a, b):
    return lax.dot_general(a, b, (((1,), (1,)), ((), ())), preferred_element_type=jnp.float32)


def work_kernel(names, pos, inverse, inverse_sib, side_own, side_sib, blocks, blocks_sib, *rest):
    arrays, rest = dict(zip(names, rest)), rest[len(names):]
    send, keep, table, sectors, right, wave, lefts, total, sem_r, sem_a, sem_b, sem_t = rest
    slots = slots_of(names)
    n = len(slots)

    tables = []
    for side, ref in enumerate((side_own, side_sib)):
        tables.append(pltpu.make_async_copy(ref.at[NM * N:], table.at[side], sem_t.at[side]))
        tables[side].start()
    core = pos[3]
    at = 0
    for name in names:
        if width(name) == 1:
            pltpu.make_async_copy(arrays[name], right.at[at], sem_r.at[at]).start()
        else:
            for t in range(width(name)):
                pltpu.make_async_copy(arrays[name].at[t], right.at[at + t], sem_r.at[at + t]).start()
        at += width(name)
    for i, slot in enumerate(slots):
        sectors[i] = sector(pos, core, slot)

    def own_copy(i):
        return pltpu.make_async_copy(blocks.at[inverse[sectors[i]]], wave.at[i, 0], sem_a.at[i])

    def sib_copy(i):
        return pltpu.make_async_copy(blocks_sib.at[inverse_sib[sectors[i]]], wave.at[i, 1], sem_b.at[i])

    def start(i, carry):
        own_copy(i).start()
        sib_copy(i).start()
        return carry

    lax.fori_loop(0, n, start, 0)
    for side, ref in enumerate((side_own, side_sib)):
        for w in range(NM):
            high, low = split(ref[w * N:(w + 1) * N])
            lefts[side, w * N:(w + 1) * N, :N] = high
            lefts[side, w * N:(w + 1) * N, N:] = low
    tables[0].wait()
    tables[1].wait()

    m = pos[0]
    zero = jnp.zeros((N, N), jnp.bfloat16)

    def step(i, carry):
        pltpu.make_async_copy(right.at[i], right.at[i], sem_r.at[i]).wait()
        own_copy(i).wait()
        sib_copy(i).wait()
        parts = []
        for side in range(2):
            high, low = split(wave[i, side])
            weights = jnp.concatenate(
                [jnp.concatenate([high, low], 1), jnp.concatenate([high, zero], 1)], 0)
            both = jnp.dot(lefts[side], weights, preferred_element_type=jnp.float32)
            both = both[:, :N] + both[:, N:]
            parts.append([split(both[w * N:(w + 1) * N] * table[side, w, sectors[i]]) for w in range(NM)])
        acc = None
        for w in range(0, NM, 2):
            high = jnp.concatenate([jnp.concatenate([parts[s][w][0], parts[s][w + 1][0]], 1) for s in range(2)], 0)
            low = jnp.concatenate([jnp.concatenate([parts[s][w][1], parts[s][w + 1][1]], 1) for s in range(2)], 0)
            r0, r1 = split(right[i, w]), split(right[i, w + 1])
            r_high = jnp.concatenate([r0[0], r1[0]], 1)
            r_low = jnp.concatenate([r0[1], r1[1]], 1)
            big = dot_nt(high, jnp.concatenate([r_high, r_low], 0))
            small = dot_nt(low, r_high)
            now = big[:, :N] + big[:, N:] + small
            acc = now if acc is None else acc + now
        total[...] = acc
        share = N // NM
        near = jnp.where(core == 0, 1, 3)
        for side in range(2):
            def rows(q):
                return total[pl.ds(pl.multiple_of(side * N + q * share, share), share), :]

            send[0, side, i] = rows(m ^ near)
            send[1, side, i] = rows(m ^ 2)
            keep[0, side, i] = rows(m)
            keep[1, side, i] = rows(m ^ near ^ 2)
        return carry

    lax.fori_loop(0, n, step, 0)


def final_kernel(batches, pos, inverse, *rest):
    out = rest[-1]
    core = pos[3]
    others = rest[-2]
    at = 0
    for b, names in enumerate(batches):
        mine, term = rest[2 * b:2 * b + 2]
        for i, slot in enumerate(slots_of(names)):
            out[inverse[sector(pos, core, slot)]] = mine[i] + term[i]
            out[inverse[sector(pos, 1 - core, slot)]] = others[at]
            at += 1


SMEM = pl.BlockSpec(memory_space=pltpu.SMEM)
VMEM = pl.BlockSpec(memory_space=pltpu.VMEM)
ANY = pl.BlockSpec(memory_space=pl.ANY)


def in_hbm(array):
    return pltpu.with_memory_space_constraint(array, pltpu.HBM)


def work(limit, names, pos, inverse, inverse_sib, side_own, side_sib, blocks, blocks_sib, got):
    n = sum(width(name) for name in names)
    arrays = [in_hbm(got[name]) if name in EARLY else got[name] for name in names]
    blocks, blocks_sib = in_hbm(blocks), in_hbm(blocks_sib)
    piece = jax.ShapeDtypeStruct((2, 2, n, N // NM, N), jnp.float32)
    return pl.pallas_call(
        functools.partial(work_kernel, names),
        out_shape=(piece,) * 2,
        in_specs=[SMEM] * 3 + [VMEM] * 2 + [ANY] * (2 + len(arrays)),
        out_specs=(VMEM,) * 2,
        scratch_shapes=[
            pltpu.SMEM((2, 8, N), jnp.float32),
            pltpu.SMEM((n,), jnp.int32),
            pltpu.VMEM((n, NM, N, N), jnp.float32),
            pltpu.VMEM((n, 2, N, N), jnp.float32),
            pltpu.VMEM((2, NM * N, 2 * N), jnp.bfloat16),
            pltpu.VMEM((2 * N, N), jnp.float32),
            pltpu.SemaphoreType.DMA((n,)),
            pltpu.SemaphoreType.DMA((n,)),
            pltpu.SemaphoreType.DMA((n,)),
            pltpu.SemaphoreType.DMA((2,)),
        ],
        compiler_params=pltpu.CompilerParams(vmem_limit_bytes=limit * 2**20),
        name="work",
    )(pos, inverse, inverse_sib, side_own, side_sib, blocks, blocks_sib, *arrays)


def finish(batches, pos, inverse, pieces):
    return pl.pallas_call(
        functools.partial(final_kernel, batches),
        out_shape=jax.ShapeDtypeStruct((NX * NZ * NC, N // NM, N), jnp.float32),
        in_specs=[SMEM, SMEM] + [VMEM] * len(pieces),
        out_specs=VMEM,
        compiler_params=pltpu.CompilerParams(vmem_limit_bytes=16 * 2**20),
        name="finish",
    )(pos, inverse, *pieces)


def shift(array, axis, step):
    size = {"x": NX, "z": NZ, "c": NC}[axis]
    return lax.ppermute(array, axis, [(i, (i + step) % size) for i in range(size)])


def place(x, z, c):
    return ((x % NX) * NZ + z % NZ) * NC + c


def by_core(array, step, cores=(0, 1)):
    pairs = []
    for x in range(NX):
        for z in range(NZ):
            pairs += [(place(x, z, c), place(x + step * c, z + step * (1 - c), c)) for c in cores]
    return lax.ppermute(array, TENSOR, pairs)


def by_core_far(array, axis, length=1):
    pairs = []
    for x in range(NX):
        for z in range(NZ):
            for c, step in ((0, length), (1, -length)):
                to = place(x + step, z, c) if axis == "x" else place(x, z + step, c)
                pairs.append((place(x, z, c), to))
    return lax.ppermute(array, TENSOR, pairs)


def fence(values):
    return lax.optimization_barrier(values)


def hops(first, second):
    return [(i * NC + c, (i ^ (first, second)[c]) * NC + c) for i in range(NM) for c in range(NC)]


def halve(parts):
    send, keep = parts
    return keep + lax.ppermute(send, ("m", "c"), hops(1, 3))


def quarter(sums):
    got = lax.ppermute(sums[1], ("m", "c"), hops(3, 1))
    return sums[0, 0], got[0], sums[0, 1] + got[1]


def direct(parts):
    send, keep = parts
    one = lax.ppermute(send[0], ("m", "c"), hops(1, 3))
    two = lax.ppermute(send[1], ("m", "c"), hops(2, 2))
    three = lax.ppermute(keep[1], ("m", "c"), hops(3, 1))
    here, there = keep[0] + one, two + three
    return here[0], there[0], here[1] + there[1]


def body(wavefunction, left_env, right_env, mpo_values, mpo_pattern, physical, right_sector, sector_size):
    m, x, z, c = (lax.axis_index(a) for a in ("m", "x", "z", "c"))
    first = c == 0
    live = jnp.arange(N, dtype=jnp.int32) < sector_size[0]
    own = jnp.where(live[:, None] & live[None, :], right_env[:, 0], 0.0)

    def pick(one, two):
        return jnp.where(first, one, two)

    got = dict(own=own)

    def tie(*names):
        for name, value in zip(names, lax.optimization_barrier([got[name] for name in names])):
            got[name] = value

    def arrive(**arrays):
        got.update(arrays)

    pos = jnp.stack([m, x, z, c]).astype(jnp.int32)
    block = jnp.arange(NC * HALF, dtype=jnp.int32)
    weights = mpo_values * mpo_pattern.astype(jnp.float32)
    is_state = physical[None, :] == jnp.arange(weights.shape[1], dtype=jnp.int32)[:, None]
    coef = jnp.sum(jnp.where(is_state[None], weights[:, :, None], 0.0), axis=1)
    is_sector = right_sector == block[None, :]
    inverse = jnp.sum(jnp.where(is_sector, block[:, None], 0), axis=0)
    coef = jnp.sum(jnp.where(is_sector[None], coef[:, :, None], 0.0), axis=1)
    table = jnp.concatenate([coef, inverse.astype(jnp.float32)[None]], axis=0)
    table = jnp.pad(table, ((0, 8 - NM - 1), (0, N - NC * HALF)))
    left = jnp.where(live[:, None] & live[None, :], left_env[:, 0], 0.0).reshape(NM * N, N)
    side = jnp.concatenate([left, table], axis=0)

    def run(batch):
        inverse_sib = got["side_sib"][NM * N + NM, :NC * HALF].astype(jnp.int32)
        return work(
            LIMITS[batch], BATCHES[batch], pos, inverse, inverse_sib, side, got["side_sib"],
            wavefunction, got["blocks_sib"], got)

    arrive(zf1=shift(own, "z", 1), zb1=shift(own, "z", -1))
    arrive(xf1=shift(own, "x", 1), xb1=shift(own, "x", -1))
    arrive(side=side, blocks_sib=shift(wavefunction, "c", 1))
    tie("zf1", "zb1", "xf1", "xb1", "side", "blocks_sib")

    zf1, zb1, xf1, xb1 = (got[name] for name in ("zf1", "zb1", "xf1", "xb1"))
    arrive(zf2=shift(zf1, "z", 1), zb2=shift(zb1, "z", -1))
    k1 = pick(jnp.stack([xf1, xb1]), jnp.stack([zf1, zb1]))
    arrive(k1f=by_core(k1, 1), k1b=by_core(k1, -1))
    arrive(side_sib=shift(got["side"], "c", 1))
    xb1, got["side_sib"] = fence((xb1, got["side_sib"]))
    arrive(x2=shift(xb1, "x", -1))
    tie("zf2", "zb2", "x2", "k1f", "k1b")

    zf2, zb2, x2, k1f, k1b = (got[name] for name in ("zf2", "zb2", "x2", "k1f", "k1b"))
    arrive(zf3=shift(zf2, "z", 1), zb3=shift(zb2, "z", -1))
    arrive(
        k2f=by_core(pick(jnp.stack([k1f[0], k1f[1], x2]), jnp.stack([zf2, zb2, k1f[0]])), 1),
        k2b=by_core(pick(jnp.stack([k1b[0], k1b[1], x2]), jnp.stack([zf2, zb2, k1b[1]])), -1),
    )
    a = got["a"] = run(0)
    tie("zf3", "zb3", "a")
    zf3, zb3 = got["zf3"], got["zb3"]
    arrive(z4=by_core_far(pick(zf3, zb3), "z"))
    tie("k2f", "k2b", "z4")

    k2f, k2b, z4 = (got[name] for name in ("k2f", "k2b", "z4"))
    arrive(df1=shift(z4, "x", 1), db1=shift(z4, "x", -1))
    arrive(
        k3f=by_core(pick(k2f, jnp.stack([zb3, k2f[0], zf3])), 1),
        k3b=by_core(pick(k2b, jnp.stack([zf3, k2b[1], zb3])), -1),
    )
    a = halve(a)
    b = got["b"] = run(1)
    tie("df1", "db1", "k3f", "k3b", "b")

    k3f, k3b = got["k3f"], got["k3b"]
    arrive(d2=shift(got["df1"], "x", 1))
    arrive(k4f=by_core(k3f[2], 1), k4b=by_core(k3b[2], -1))
    d = got["d"] = run(2)
    b = halve(b)
    a = quarter(a)
    tie("d2", "k4f", "k4b", "d")

    e = run(3)
    d = halve(got["d"])
    b, d, e = fence((b, d, e))

    e = direct(e)
    b = quarter(b)
    d = quarter(d)
    a, b, d, e = fence((a, b, d, e))
    others = shift(jnp.concatenate([part[2] for part in (a, b, d, e)]), "c", 1)
    return finish(BATCHES, pos, inverse, a[:2] + b[:2] + d[:2] + e[:2] + (others,))


def solution(mesh):
    grid = Mesh(mesh.devices.reshape(NM, NX, NZ, NC), ("m", "x", "z", "c"))
    in_specs = (
        P(TENSOR, None, None),
        P("m", TENSOR, None, None),
        P("m", TENSOR, None, None),
        P("m", None),
        P("m", None),
        P(TENSOR),
        P(TENSOR, None),
        P(TENSOR),
    )
    out_specs = P(TENSOR, "m", None)
    return jax.shard_map(body, mesh=grid, in_specs=in_specs, out_specs=out_specs, check_vma=False)
```

```python
import functools

import jax
import jax.numpy as jnp
from jax import lax
from jax.experimental import pallas as pl
from jax.experimental.pallas import tpu as pltpu
from jax.sharding import Mesh
from jax.sharding import PartitionSpec as P

NX, NZ, NC, NM = 4, 8, 2, 4
N = 128
TENSOR = ("x", "z", "c")
HALF = NX * NZ

SYM = dict(
    own=(0, 0), zf1=(0, -1), zb1=(0, 1), zf2=(0, -2), zb2=(0, 2), zf3=(0, -3), zb3=(0, 3), z4=(0, 4),
    xf1=(-1, 0), xb1=(1, 0), x2=(2, 0), df1=(-1, 4), db1=(1, 4), d2=(2, 4),
)
STEPS = dict(
    k1f=([(-1, -1), (1, -1)], [(-1, -1), (-1, 1)]),
    k1b=([(-1, 1), (1, 1)], [(1, -1), (1, 1)]),
    k2f=([(-1, -2), (1, -2), (2, -1)], [(-1, -2), (-1, 2), (-2, -1)]),
    k2b=([(-1, 2), (1, 2), (2, 1)], [(1, -2), (1, 2), (2, 1)]),
    k3f=([(-1, -3), (1, -3), (2, -2)], [(-1, 3), (-2, -2), (-1, -3)]),
    k3b=([(-1, 3), (1, 3), (2, 2)], [(1, -3), (2, 2), (1, 3)]),
    k4f=([(2, -3)], [(-2, -3)]),
    k4b=([(2, 3)], [(2, 3)]),
)
BATCHES = (
    ("own", "zf1", "zb1", "xf1", "xb1", "zf2", "zb2", "x2", "k1f", "k1b"),
    ("zf3", "zb3", "z4", "k2f", "k2b"),
    ("k3f", "k3b", "df1", "db1"),
    ("k4f", "k4b", "d2"),
)

EARLY = ("own", "zf1", "zb1", "xf1", "xb1", "x2", "zf2", "zb2", "k1f", "k1b")


def slots_of(names):
    slots = []
    for name in names:
        slots += [(SYM[name], SYM[name])] if name in SYM else list(zip(*STEPS[name]))
    return slots


def width(name):
    return 1 if name in SYM else len(STEPS[name][0])


def sector(pos, core, slot):
    (x0, z0), (x1, z1) = slot
    first = core == 0
    x = (pos[1] + jnp.where(first, x0 % NX, x1 % NX)) % NX
    z = (pos[2] + jnp.where(first, z0 % NZ, z1 % NZ)) % NZ
    return (x * NZ + z) * NC + core


def split(value):
    high = value.astype(jnp.bfloat16)
    return high, (value - high.astype(jnp.float32)).astype(jnp.bfloat16)


def dot_nt(a, b):
    return lax.dot_general(a, b, (((1,), (1,)), ((), ())), preferred_element_type=jnp.float32)


def work_kernel(first, names, pos, inverse, inverse_sib, side_own, side_sib, blocks, blocks_sib, *rest):
    if not first:
        lefts, rest = rest[0], rest[1:]
    arrays, rest = dict(zip(names, rest)), rest[len(names):]
    send, keep, *rest = rest
    if first:
        lefts, rest = rest[0], rest[1:]
    table, sectors, right, wave, total, sem_r, sem_a, sem_b, sem_t = rest
    slots = slots_of(names)
    n = len(slots)

    tables = []
    for side, ref in enumerate((side_own, side_sib)):
        tables.append(pltpu.make_async_copy(ref.at[NM * N:], table.at[side], sem_t.at[side]))
        tables[side].start()
    core = pos[3]
    at = 0
    for name in names:
        if width(name) == 1:
            pltpu.make_async_copy(arrays[name], right.at[at], sem_r.at[at]).start()
        else:
            for t in range(width(name)):
                pltpu.make_async_copy(arrays[name].at[t], right.at[at + t], sem_r.at[at + t]).start()
        at += width(name)
    for i, slot in enumerate(slots):
        sectors[i] = sector(pos, core, slot)

    def own_copy(i):
        return pltpu.make_async_copy(blocks.at[inverse[sectors[i]]], wave.at[i, 0], sem_a.at[i])

    def sib_copy(i):
        return pltpu.make_async_copy(blocks_sib.at[inverse_sib[sectors[i]]], wave.at[i, 1], sem_b.at[i])

    def start(i, carry):
        own_copy(i).start()
        sib_copy(i).start()
        return carry

    lax.fori_loop(0, n, start, 0)
    if first:
        for side, ref in enumerate((side_own, side_sib)):
            for w in range(NM):
                high, low = split(ref[w * N:(w + 1) * N])
                lefts[side, w * N:(w + 1) * N, :N] = high
                lefts[side, w * N:(w + 1) * N, N:] = low
    tables[0].wait()
    tables[1].wait()

    m = pos[0]
    zero = jnp.zeros((N, N), jnp.bfloat16)

    def step(i, carry):
        pltpu.make_async_copy(right.at[i], right.at[i], sem_r.at[i]).wait()
        own_copy(i).wait()
        sib_copy(i).wait()
        parts = []
        for side in range(2):
            high, low = split(wave[i, side])
            weights = jnp.concatenate(
                [jnp.concatenate([high, low], 1), jnp.concatenate([high, zero], 1)], 0)
            both = jnp.dot(lefts[side], weights, preferred_element_type=jnp.float32)
            both = both[:, :N] + both[:, N:]
            parts.append([split(both[w * N:(w + 1) * N] * table[side, w, sectors[i]]) for w in range(NM)])
        acc = None
        for w in range(0, NM, 2):
            high = jnp.concatenate([jnp.concatenate([parts[s][w][0], parts[s][w + 1][0]], 1) for s in range(2)], 0)
            low = jnp.concatenate([jnp.concatenate([parts[s][w][1], parts[s][w + 1][1]], 1) for s in range(2)], 0)
            r0, r1 = split(right[i, w]), split(right[i, w + 1])
            r_high = jnp.concatenate([r0[0], r1[0]], 1)
            r_low = jnp.concatenate([r0[1], r1[1]], 1)
            big = dot_nt(high, jnp.concatenate([r_high, r_low], 0))
            small = dot_nt(low, r_high)
            now = big[:, :N] + big[:, N:] + small
            acc = now if acc is None else acc + now
        total[...] = acc
        share = N // NM
        near = jnp.where(core == 0, 1, 3)
        for side in range(2):
            def rows(q):
                return total[pl.ds(pl.multiple_of(side * N + q * share, share), share), :]

            send[0, side, i] = rows(m ^ near)
            send[1, side, i] = rows(m ^ 2)
            keep[0, side, i] = rows(m)
            keep[1, side, i] = rows(m ^ near ^ 2)
        return carry

    lax.fori_loop(0, n, step, 0)


def final_kernel(batches, pos, inverse, *rest):
    out = rest[-1]
    core = pos[3]
    others = rest[-2]
    at = 0
    for b, names in enumerate(batches):
        mine, term = rest[2 * b:2 * b + 2]
        for i, slot in enumerate(slots_of(names)):
            out[inverse[sector(pos, core, slot)]] = mine[i] + term[i]
            out[inverse[sector(pos, 1 - core, slot)]] = others[at]
            at += 1


SMEM = pl.BlockSpec(memory_space=pltpu.SMEM)
VMEM = pl.BlockSpec(memory_space=pltpu.VMEM)
ANY = pl.BlockSpec(memory_space=pl.ANY)


def in_hbm(array):
    return pltpu.with_memory_space_constraint(array, pltpu.HBM)


def work(names, pos, inverse, inverse_sib, side_own, side_sib, blocks, blocks_sib, got, lefts):
    first = lefts is None
    given = [] if first else [lefts]
    n = sum(width(name) for name in names)
    arrays = [in_hbm(got[name]) if name in EARLY else got[name] for name in names]
    blocks, blocks_sib = in_hbm(blocks), in_hbm(blocks_sib)
    piece = jax.ShapeDtypeStruct((2, 2, n, N // NM, N), jnp.float32)
    return pl.pallas_call(
        functools.partial(work_kernel, first, names),
        out_shape=(piece,) * 2 + (jax.ShapeDtypeStruct((2, NM * N, 2 * N), jnp.bfloat16),) * first,
        in_specs=[SMEM] * 3 + [VMEM if first else ANY] * 2 + [ANY] * 2 + [VMEM] * (not first) + [ANY] * len(arrays),
        out_specs=(VMEM,) * (2 + first),
        scratch_shapes=[
            pltpu.SMEM((2, 8, N), jnp.float32),
            pltpu.SMEM((n,), jnp.int32),
            pltpu.VMEM((n, NM, N, N), jnp.float32),
            pltpu.VMEM((n, 2, N, N), jnp.float32),
            pltpu.VMEM((2 * N, N), jnp.float32),
            pltpu.SemaphoreType.DMA((n,)),
            pltpu.SemaphoreType.DMA((n,)),
            pltpu.SemaphoreType.DMA((n,)),
            pltpu.SemaphoreType.DMA((2,)),
        ],
        compiler_params=pltpu.CompilerParams(vmem_limit_bytes=12 * 2**20),
        name="work",
    )(pos, inverse, inverse_sib, side_own, side_sib, blocks, blocks_sib, *given, *arrays)


def finish(batches, pos, inverse, pieces):
    return pl.pallas_call(
        functools.partial(final_kernel, batches),
        out_shape=jax.ShapeDtypeStruct((NX * NZ * NC, N // NM, N), jnp.float32),
        in_specs=[SMEM, SMEM] + [VMEM] * len(pieces),
        out_specs=VMEM,
        compiler_params=pltpu.CompilerParams(vmem_limit_bytes=16 * 2**20),
        name="finish",
    )(pos, inverse, *pieces)


def shift(array, axis, step):
    size = {"x": NX, "z": NZ, "c": NC}[axis]
    return lax.ppermute(array, axis, [(i, (i + step) % size) for i in range(size)])


def place(x, z, c):
    return ((x % NX) * NZ + z % NZ) * NC + c


def by_core(array, step, cores=(0, 1)):
    pairs = []
    for x in range(NX):
        for z in range(NZ):
            pairs += [(place(x, z, c), place(x + step * c, z + step * (1 - c), c)) for c in cores]
    return lax.ppermute(array, TENSOR, pairs)


def by_core_far(array, axis, length=1):
    pairs = []
    for x in range(NX):
        for z in range(NZ):
            for c, step in ((0, length), (1, -length)):
                to = place(x + step, z, c) if axis == "x" else place(x, z + step, c)
                pairs.append((place(x, z, c), to))
    return lax.ppermute(array, TENSOR, pairs)


def fence(values):
    return lax.optimization_barrier(values)


def hops(first, second):
    return [(i * NC + c, (i ^ (first, second)[c]) * NC + c) for i in range(NM) for c in range(NC)]


def halve(parts):
    send, keep = parts
    return keep + lax.ppermute(send, ("m", "c"), hops(1, 3))


def quarter(sums):
    got = lax.ppermute(sums[1], ("m", "c"), hops(3, 1))
    return sums[0, 0], got[0], sums[0, 1] + got[1]


def direct(parts):
    send, keep = parts
    one = lax.ppermute(send[0], ("m", "c"), hops(1, 3))
    two = lax.ppermute(send[1], ("m", "c"), hops(2, 2))
    three = lax.ppermute(keep[1], ("m", "c"), hops(3, 1))
    here, there = keep[0] + one, two + three
    return here[0], there[0], here[1] + there[1]


def body(wavefunction, left_env, right_env, mpo_values, mpo_pattern, physical, right_sector, sector_size):
    m, x, z, c = (lax.axis_index(a) for a in ("m", "x", "z", "c"))
    first = c == 0
    live = jnp.arange(N, dtype=jnp.int32) < sector_size[0]
    own = jnp.where(live[:, None] & live[None, :], right_env[:, 0], 0.0)

    def pick(one, two):
        return jnp.where(first, one, two)

    got = dict(own=own)

    def tie(*names):
        for name, value in zip(names, lax.optimization_barrier([got[name] for name in names])):
            got[name] = value

    def arrive(**arrays):
        got.update(arrays)

    pos = jnp.stack([m, x, z, c]).astype(jnp.int32)
    block = jnp.arange(NC * HALF, dtype=jnp.int32)
    weights = mpo_values * mpo_pattern.astype(jnp.float32)
    is_state = physical[None, :] == jnp.arange(weights.shape[1], dtype=jnp.int32)[:, None]
    coef = jnp.sum(jnp.where(is_state[None], weights[:, :, None], 0.0), axis=1)
    is_sector = right_sector == block[None, :]
    inverse = jnp.sum(jnp.where(is_sector, block[:, None], 0), axis=0)
    coef = jnp.sum(jnp.where(is_sector[None], coef[:, :, None], 0.0), axis=1)
    table = jnp.concatenate([coef, inverse.astype(jnp.float32)[None]], axis=0)
    table = jnp.pad(table, ((0, 8 - NM - 1), (0, N - NC * HALF)))
    left = jnp.where(live[:, None] & live[None, :], left_env[:, 0], 0.0).reshape(NM * N, N)
    side = jnp.concatenate([left, table], axis=0)

    def run(batch, lefts=None):
        inverse_sib = got["side_sib"][NM * N + NM, :NC * HALF].astype(jnp.int32)
        return work(
            BATCHES[batch], pos, inverse, inverse_sib, side, got["side_sib"],
            wavefunction, got["blocks_sib"], got, lefts)

    arrive(zf1=shift(own, "z", 1), zb1=shift(own, "z", -1))
    arrive(xf1=shift(own, "x", 1), xb1=shift(own, "x", -1))
    arrive(side=side, blocks_sib=shift(wavefunction, "c", 1))
    tie("zf1", "zb1", "xf1", "xb1", "side", "blocks_sib")

    zf1, zb1, xf1, xb1 = (got[name] for name in ("zf1", "zb1", "xf1", "xb1"))
    arrive(zf2=shift(zf1, "z", 1), zb2=shift(zb1, "z", -1))
    k1 = pick(jnp.stack([xf1, xb1]), jnp.stack([zf1, zb1]))
    arrive(k1f=by_core(k1, 1), k1b=by_core(k1, -1))
    arrive(side_sib=shift(got["side"], "c", 1))
    xb1, got["side_sib"] = fence((xb1, got["side_sib"]))
    arrive(x2=shift(xb1, "x", -1))
    tie("zf2", "zb2", "x2", "k1f", "k1b")

    zf2, zb2, x2, k1f, k1b = (got[name] for name in ("zf2", "zb2", "x2", "k1f", "k1b"))
    arrive(zf3=shift(zf2, "z", 1), zb3=shift(zb2, "z", -1))
    arrive(
        k2f=by_core(pick(jnp.stack([k1f[0], k1f[1], x2]), jnp.stack([zf2, zb2, k1f[0]])), 1),
        k2b=by_core(pick(jnp.stack([k1b[0], k1b[1], x2]), jnp.stack([zf2, zb2, k1b[1]])), -1),
    )
    *a, lefts = run(0)
    got["a"] = a
    tie("zf3", "zb3", "a")
    zf3, zb3 = got["zf3"], got["zb3"]
    arrive(z4=by_core_far(pick(zf3, zb3), "z"))
    tie("k2f", "k2b", "z4")

    k2f, k2b, z4 = (got[name] for name in ("k2f", "k2b", "z4"))
    arrive(df1=shift(z4, "x", 1), db1=shift(z4, "x", -1))
    arrive(
        k3f=by_core(pick(k2f, jnp.stack([zb3, k2f[0], zf3])), 1),
        k3b=by_core(pick(k2b, jnp.stack([zf3, k2b[1], zb3])), -1),
    )
    a = halve(a)
    b = got["b"] = run(1, lefts)
    tie("df1", "db1", "k3f", "k3b", "b")

    k3f, k3b = got["k3f"], got["k3b"]
    arrive(d2=shift(got["df1"], "x", 1))
    arrive(k4f=by_core(k3f[2], 1), k4b=by_core(k3b[2], -1))
    d = got["d"] = run(2, lefts)
    b = halve(b)
    a = quarter(a)
    tie("d2", "k4f", "k4b", "d")

    e = run(3, lefts)
    d = halve(got["d"])
    b, d, e = fence((b, d, e))

    e = direct(e)
    b = quarter(b)
    d = quarter(d)
    a, b, d, e = fence((a, b, d, e))
    others = shift(jnp.concatenate([part[2] for part in (a, b, d, e)]), "c", 1)
    return finish(BATCHES, pos, inverse, a[:2] + b[:2] + d[:2] + e[:2] + (others,))


def solution(mesh):
    grid = Mesh(mesh.devices.reshape(NM, NX, NZ, NC), ("m", "x", "z", "c"))
    in_specs = (
        P(TENSOR, None, None),
        P("m", TENSOR, None, None),
        P("m", TENSOR, None, None),
        P("m", None),
        P("m", None),
        P(TENSOR),
        P(TENSOR, None),
        P(TENSOR),
    )
    out_specs = P(TENSOR, "m", None)
    return jax.shard_map(body, mesh=grid, in_specs=in_specs, out_specs=out_specs, check_vma=False)
```
